256 devices in a mesh: ctx: 16 (over z_hi, y, core), dp: 16 (over x, z_lo).
Axes of the slice: x: 4, y: 4, z: 8 (z_hi: 2, z_lo: 4; z = z_hi * 4 + z_lo), core: 2. Of those that a mesh axis runs over, the one named last changes fastest.
Arguments:
- queries: bfloat16 [16, 2048, 4096], P('dp', 'ctx'), may hold values from -180 to 180
- keys: bfloat16 [16, 2048, 512], P('dp', 'ctx'), may hold values from -18 to 18
- values: bfloat16 [16, 2048, 512], P('dp', 'ctx'), may hold values from -6 to 6
- grad_out: bfloat16 [16, 2048, 4096], P('dp', 'ctx'), may hold values from -6 to 6
- doc_lengths: int32 [16, 16], P('dp'), may hold values from 1 to 256, 2048 in all within a row
- placement: int32 [16, 16, 16], P('dp'), may hold values from 0 to 15, each once within a row
Outputs:
- attn_out: bfloat16 [16, 2048, 4096], P('dp', 'ctx')
- grad_q: bfloat16 [16, 2048, 4096], P('dp', 'ctx')
- grad_k: bfloat16 [16, 2048, 512], P('dp', 'ctx')
- grad_v: bfloat16 [16, 2048, 512], P('dp', 'ctx')
- grad_bias: float32 [5120], replicated
The draws below stay inside these ranges and needn't reach their ends.
Inputs may be any that keep to these rules, and one draw needn't show every extreme that they name: `doc_lengths`: each row sums to 2048, and its longest document has exactly 256 rows. placement[b, s, j] is the device that works on block j (rows j * 8 to j * 8 + 7) of device s's 128 rows; each placement[b, s] is a permutation of 0 to 15.
All inputs are finite; a program needn't handle non-finite values.
Results may differ from the reference program's by a relative error of at most 0.0095.
Values may be sent and summed in bfloat16 or wider, within the bound.
A program may use at most 128 MiB of HBM per device.

```python
import math
import jax
import jax.numpy as jnp
import numpy as np
from jax import lax

HD = 128
HQ = 32
HK = 4
TOK_DEV = 128
QW = 4096
KW = 512
SEQ = 2048
BLK = 8
DOC_MOST = 256
NDOC = 16
N_CTX = 16
N_DP = 16


def drawn_rows(key, low, high):
    base = jnp.clip(jax.random.normal(key, (N_DP, SEQ, KW), jnp.float32), -6.0, 6.0)
    spread = jax.random.uniform(jax.random.fold_in(key, 1), (N_DP, SEQ, 1), jnp.float32, math.log(low), math.log(high))
    positions = jnp.arange(SEQ)
    marks = (positions % 97 == 5) | (positions % 97 == 4)
    row_scale = jnp.where(marks[None, :, None], 1.0, jnp.exp(spread))
    return base * row_scale


def draw_keys(key, part):
    shared = drawn_rows(key, 1.0, 1.0)
    result = shared
    return result.astype(jnp.bfloat16)


def draw_queries(key, part):
    key = jax.random.fold_in(key, 5)
    result = jnp.clip(jax.random.normal(key, (N_DP, SEQ, QW), jnp.float32), -6.0, 6.0)
    return result.astype(jnp.bfloat16)


def block_scale(stream_key, dims, split, least, largest):
    def one(axis_at, blocks):
        heights = jax.random.uniform(jax.random.fold_in(jax.random.fold_in(stream_key, 6), axis_at), (blocks,), jnp.float32, least / len(split), largest / len(split))
        return jnp.repeat(jnp.exp(heights), dims[axis_at] // blocks).reshape((-1,) + (1,) * (len(dims) - axis_at - 1))

    loudness = one(*split[0])
    for cut in split[1:]:
        loudness = loudness * one(*cut)
    return loudness


def length_profile(amount, total, reach, skew):
    loads = [(1 << 20) // math.isqrt(rank ** skew) + 1 for rank in range(2, amount + 1)]
    rest, holding = total - reach - (amount - 1), [1] * (amount - 1)
    while rest > 0:
        movable = [i for i in range(amount - 1) if holding[i] < reach]
        whole, budget = sum([loads[i] for i in movable]), rest
        for i in movable:
            addition = min(reach - holding[i], max(1, budget * loads[i] // whole), rest)
            holding[i] = holding[i] + addition
            rest = rest - addition
    return np.array([reach] + holding)


def uneven(stream_key, count, total, limit, lean):
    if count == 2:
        one = jax.random.randint(stream_key, (), max(1, total - limit), min(limit, total - 1) + 1)
        return jnp.stack([one, total - one])
    sizes = jnp.asarray(length_profile(count, total, limit, lean), jnp.int32)
    couples = (count - 1) // 2
    giver, receiver = sizes[1:1 + 2 * couples:2], sizes[2:2 + 2 * couples:2]
    slack = jnp.minimum(giver - 1, limit - receiver)
    passed = jax.random.randint(jax.random.fold_in(stream_key, 1), (couples,), 0, 1 << 20) % (slack + 1)
    sizes = sizes.at[1:1 + 2 * couples:2].set(giver - passed).at[2:2 + 2 * couples:2].set(receiver + passed)
    return sizes[jax.random.permutation(jax.random.fold_in(stream_key, 2), count)]


def bell_draw(rng, dims, deviation, bound, shards=(), kind=jnp.bfloat16):
    values = deviation * jax.random.normal(rng, dims, jnp.float32)
    if shards:
        values = values * block_scale(rng, dims, shards, -0.22, 0.18)
    return jnp.clip(values, -bound, bound).astype(kind)


def setup_inputs(seed: int = 0) -> dict:
    splits = jax.random.split(jax.random.key(seed), 7)
    return {
        "queries": draw_queries(jax.random.fold_in(splits[6], 71), 0),
        "keys": draw_keys(jax.random.fold_in(splits[6], 71), 0),
        "values": bell_draw(splits[2], (N_DP, SEQ, KW), 1.0, 6.0, ((0, 16), (1, 16))),
        "grad_out": bell_draw(splits[3], (N_DP, SEQ, QW), 1.0, 6.0, ((0, 16), (1, 16))),
        "doc_lengths": jax.vmap(lambda own: uneven(own, NDOC, SEQ, DOC_MOST, 2))(jax.random.split(splits[4], N_DP)).reshape((N_DP, NDOC)).astype(jnp.int32),
        "placement": jax.vmap(lambda own: jax.random.permutation(own, N_CTX))(jax.random.split(splits[5], N_DP * N_CTX)).reshape((N_DP, N_CTX, N_CTX)).astype(jnp.int32),
    }


def doc_index(starts, positions):
    return lax.optimization_barrier(jnp.sum((starts[None, :] <= positions[:, None]).astype(jnp.int32), axis=1)) - 1

def block_attention(query_block, dout_block, key_window, value_window, query_pos, query_doc, key_pos, key_doc):
    row_count = query_block.shape[0]
    key_count = key_window.shape[0]
    group_size = HQ // HK
    score_scale = 1.0 / math.sqrt(HD)
    query_heads = query_block.astype(jnp.float32).reshape(row_count, HK, group_size, HD)
    dout_heads = dout_block.astype(jnp.float32).reshape(row_count, HK, group_size, HD)
    key_heads = key_window.astype(jnp.float32).reshape(key_count, HK, HD)
    value_heads = value_window.astype(jnp.float32).reshape(key_count, HK, HD)
    scores = jnp.einsum('rgnd,wgd->gnrw', query_heads, key_heads) * score_scale
    allowed = (query_doc[:, None] == key_doc[None, :]) & (key_pos[None, :] <= query_pos[:, None])
    scores = jnp.where(allowed, scores, -1e+30)
    row_top = lax.optimization_barrier(jnp.max(scores, axis=-1, keepdims=True))
    exponents = jnp.where(allowed, jnp.exp(scores - row_top), 0.0)
    probs = exponents / lax.optimization_barrier(jnp.sum(exponents, axis=-1, keepdims=True))
    weights = lax.optimization_barrier(probs.astype(jnp.bfloat16)).astype(jnp.float32)
    context = jnp.einsum('gnrw,wgd->rgnd', weights, value_heads)
    delta_sum = lax.optimization_barrier(jnp.sum(dout_heads * context, axis=3))
    prob_grad = jnp.einsum('rgnd,wgd->gnrw', dout_heads, value_heads)
    score_grad = probs * (prob_grad - jnp.transpose(delta_sum, (1, 2, 0))[..., None]) * score_scale
    score_grad = lax.optimization_barrier(score_grad.astype(jnp.bfloat16)).astype(jnp.float32)
    query_grad = jnp.einsum('gnrw,wgd->rgnd', score_grad, key_heads).reshape(row_count, -1)
    key_grad = jnp.einsum('gnrw,rgnd->wgd', score_grad, query_heads).reshape(key_count, -1)
    value_grad = jnp.einsum('gnrw,rgnd->wgd', weights, dout_heads).reshape(key_count, -1)
    return (context.reshape(row_count, -1), query_grad, key_grad, value_grad)

def reference(queries, keys, values, grad_out, doc_lengths, placement):
    full_width = DOC_MOST + TOK_DEV

    def one_sequence(inputs):
        query_rows, key_rows, value_rows, dout_rows, lengths = inputs
        starts = (jnp.cumsum(lengths) - lengths).astype(jnp.int32)

        def block_step(totals, block_index):
            block_start = (block_index * TOK_DEV).astype(jnp.int32)
            window_start = jnp.clip(block_start + TOK_DEV - full_width, 0, SEQ - full_width).astype(jnp.int32)
            query_block = lax.dynamic_slice_in_dim(query_rows, block_start, TOK_DEV, 0)
            dout_block = lax.dynamic_slice_in_dim(dout_rows, block_start, TOK_DEV, 0)
            key_window = lax.dynamic_slice_in_dim(key_rows, window_start, full_width, 0)
            value_window = lax.dynamic_slice_in_dim(value_rows, window_start, full_width, 0)
            query_pos = block_start + jnp.arange(TOK_DEV, dtype=jnp.int32)
            key_pos = window_start + jnp.arange(full_width, dtype=jnp.int32)
            context, query_grad, key_grad, value_grad = block_attention(query_block, dout_block, key_window, value_window, query_pos, doc_index(starts, query_pos), key_pos, doc_index(starts, key_pos))
            key_total = lax.dynamic_update_slice_in_dim(totals[0], lax.dynamic_slice_in_dim(totals[0], window_start, full_width, 0) + key_grad, window_start, 0)
            value_total = lax.dynamic_update_slice_in_dim(totals[1], lax.dynamic_slice_in_dim(totals[1], window_start, full_width, 0) + value_grad, window_start, 0)
            return ((key_total, value_total), (context.astype(jnp.bfloat16), query_grad.astype(jnp.bfloat16), lax.optimization_barrier(jnp.sum(query_grad, axis=0))))
        empty_terms = jnp.zeros((SEQ, KW), jnp.float32)
        totals, outputs = lax.scan(block_step, (empty_terms, empty_terms), jnp.arange(N_CTX, dtype=jnp.int32))
        key_total, value_total = totals
        contexts, query_grads, query_sums = outputs
        bias_part = jnp.concatenate([lax.optimization_barrier(jnp.sum(query_sums, axis=0)), lax.optimization_barrier(jnp.sum(key_total, axis=0)), lax.optimization_barrier(jnp.sum(value_total, axis=0))])
        return (contexts.reshape(SEQ, QW), query_grads.reshape(SEQ, QW), key_total.astype(jnp.bfloat16), value_total.astype(jnp.bfloat16), bias_part)
    contexts, query_grads, key_grads, value_grads, bias_parts = lax.map(one_sequence, (queries, keys, values, grad_out, doc_lengths))
    grad_bias = lax.optimization_barrier(jnp.sum(bias_parts, axis=0))
    devices_iota = jnp.arange(N_CTX, dtype=jnp.int32)
    source_block = lax.optimization_barrier(jnp.sum(jnp.where(placement[:, :, :, None] == devices_iota[None, None, None, :], devices_iota[None, None, :, None], 0), axis=2)).astype(jnp.int32)

    def to_placed(row_array):
        home_blocks = row_array.reshape(N_DP, N_CTX, N_CTX, BLK, -1)
        picked = jnp.take_along_axis(home_blocks, source_block[:, :, :, None, None], axis=2)
        return jnp.transpose(picked, (0, 2, 1, 3, 4)).reshape(N_DP, SEQ, -1)
    return (to_placed(contexts), to_placed(query_grads), key_grads, value_grads, grad_bias)
```

```python
import math

import jax
import jax.numpy as jnp
from jax import lax
from jax.experimental import pallas as pl
from jax.experimental.pallas import tpu as pltpu
from jax.sharding import PartitionSpec as P

HD = 128
HQ = 32
HK = 4
GROUP = HQ // HK
ROWS = 128
WIN = 384
BLK = 8
N = 16
MESH = pl.DeviceIdType.MESH
NT = (((1,), (1,)), ((), ()))
SCALE = 1.0 / math.sqrt(HD)
LOG2E = math.log2(math.e)
SLICES = HK + 1


def dot(a, b):
    return jnp.dot(a, b, preferred_element_type=jnp.float32)


def dot_nt(a, b):
    return lax.dot_general(a, b, NT, preferred_element_type=jnp.float32)


def halves(x):
    high = x.astype(jnp.bfloat16)
    return high, (x - high.astype(jnp.float32)).astype(jnp.bfloat16)


def kernel(
    len_ref, place_ref, q_ref, k_ref, v_ref, do_ref,
    rows_ref, gk_ref, gv_ref, bias_ref,
    win, send, perm, mask, probs, dscore, ones, part, part_in, own, colsum, bvec, b1, b2, btot,
    halo_s, halo_r, a2a_s, a2a_r, loc_s, part_s, part_r, p1_s, p1_r, p2_s, p2_r, p3_s, p3_r,
):
    me = lax.axis_index("ctx")
    seq = lax.axis_index("dp")
    half = me // 8
    inner = lax.rem(me, 8)

    peers = [(1 - half) * 8 + lax.rem(inner + j, 8) for j in range(8)]
    peers += [half * 8 + lax.rem(inner + j, 8) for j in range(1, 8)]
    seqs = [lax.rem(seq + j, N) for j in range(1, N)]

    def remote(src, dst, send_sem, recv_sem, device):
        return pltpu.make_async_remote_copy(
            src_ref=src, dst_ref=dst, send_sem=send_sem, recv_sem=recv_sem,
            device_id=device, device_id_type=MESH,
        )

    barrier = pltpu.get_barrier_semaphore()
    for p in peers:
        pl.semaphore_signal(barrier, inc=1, device_id={"ctx": p}, device_id_type=MESH)
    for s in seqs:
        pl.semaphore_signal(barrier, inc=1, device_id={"dp": s}, device_id_type=MESH)

    for g in range(HK):
        win[g, 2, 0] = k_ref[:, g * HD : (g + 1) * HD]
        win[g, 2, 1] = v_ref[:, g * HD : (g + 1) * HD]

    @pl.when(me < 2)
    def _():
        win[:, 0] = jnp.zeros((HK, 2, ROWS, HD), jnp.bfloat16)

    @pl.when(me < 1)
    def _():
        win[:, 1] = jnp.zeros((HK, 2, ROWS, HD), jnp.bfloat16)

    lane = lax.broadcasted_iota(jnp.int32, (1, ROWS), 1)
    pos = me * ROWS + lane
    first = jnp.zeros((1, ROWS), jnp.int32)
    start = len_ref[0, 0] * 0
    for i in range(N):
        first = jnp.where(pos >= start, start, first)
        start = start + len_ref[0, i]
    t_pos = (me - 2) * ROWS + lax.broadcasted_iota(jnp.int32, (WIN, ROWS), 0)
    seen = (t_pos >= first) & (t_pos <= pos)
    mask[...] = jnp.where(seen, 0.0, -1e30)

    target = lax.rem(lane, BLK)
    for j in range(N):
        target = target + jnp.where(lane // BLK == j, place_ref[0, me, j] * BLK, 0)
    row = lax.broadcasted_iota(jnp.int32, (ROWS, ROWS), 0)
    perm[...] = jnp.where(row == target, 1.0, 0.0).astype(jnp.bfloat16)
    ones[...] = jnp.where(
        lax.broadcasted_iota(jnp.int32, (GROUP * ROWS, HD), 0) // ROWS
        == lax.broadcasted_iota(jnp.int32, (GROUP * ROWS, HD), 1),
        1.0, 0.0,
    ).astype(jnp.bfloat16)

    pl.semaphore_wait(barrier, len(peers) + len(seqs))

    def halo(g, slot):
        return remote(
            win.at[g, 2], win.at[g, slot], halo_s.at[g, slot], halo_r.at[g, slot],
            {"ctx": lax.rem(me + (2 - slot), N)},
        )

    def term(g, slot):
        return remote(
            part.at[g, slot], part_in.at[g, slot], part_s.at[g, slot], part_r.at[g, slot],
            {"ctx": lax.rem(me + N - (2 - slot), N)},
        )

    for g in range(HK):
        for slot in (1, 0):

            @pl.when(me + (2 - slot) < N)
            def _():
                halo(g, slot).start()

    def placed(g, p):
        cols = pl.ds(pl.multiple_of(g * GROUP * HD, GROUP * HD), GROUP * HD)
        return remote(
            send.at[p, :, :, cols], rows_ref.at[me, :, :, cols], a2a_s.at[g, p], a2a_r.at[g, me],
            {"ctx": p},
        )

    def arrived(g, p):
        cols = pl.ds(pl.multiple_of(g * GROUP * HD, GROUP * HD), GROUP * HD)
        return remote(
            send.at[p, :, :, cols], rows_ref.at[p, :, :, cols], a2a_s.at[g, p], a2a_r.at[g, p],
            {"ctx": p},
        )

    def kept(g):
        cols = pl.ds(pl.multiple_of(g * GROUP * HD, GROUP * HD), GROUP * HD)
        return pltpu.make_async_copy(
            send.at[me, :, :, cols], rows_ref.at[me, :, :, cols], loc_s.at[g]
        )

    def to_owner(s):
        return remote(bvec.at[s], b1.at[me], p1_s.at[s], p1_r.at[me], {"ctx": s})

    def group_step(g, carry):
        for slot in (1, 0):

            @pl.when(me >= 2 - slot)
            def _():
                halo(g, slot).wait_recv()

        keys = win[g, :, 0].reshape(WIN, HD)
        values = win[g, :, 1].reshape(WIN, HD)
        keys_t = keys.astype(jnp.float32).T.astype(jnp.bfloat16)
        values_t = values.astype(jnp.float32).T.astype(jnp.bfloat16)
        shut = jnp.concatenate([mask[...], mask[...]], axis=1)

        def stacked(ref, first_head, count):
            cols = pl.ds(pl.multiple_of((g * GROUP + first_head) * HD, HD), count * HD)
            x = ref[:, cols]
            return jnp.concatenate([x[:, i * HD : (i + 1) * HD] for i in range(count)], axis=0)

        for pair in range(GROUP // 2):
            q2 = stacked(q_ref, pair * 2, 2)
            do2 = stacked(do_ref, pair * 2, 2)
            scores = dot_nt(keys, q2) + shut
            top = jnp.max(scores, axis=0, keepdims=True)
            e = jnp.exp2((scores - top) * (SCALE * LOG2E))
            inv = 1.0 / jnp.sum(e, axis=0, keepdims=True)
            weights = (e * inv).astype(jnp.bfloat16)
            grad = dot_nt(values, do2)
            delta = jnp.sum(weights.astype(jnp.float32) * grad, axis=0, keepdims=True)
            ds = (e * (inv * SCALE) * (grad - delta)).astype(jnp.bfloat16)
            at = slice(pair * 2 * ROWS, (pair + 1) * 2 * ROWS)
            probs[:, at] = weights
            dscore[:, at] = ds
            cols = pl.ds(pl.multiple_of((g * GROUP + pair * 2) * HD, 2 * HD), 2 * HD)
            for i, out_t in enumerate((dot(values_t, weights), dot(keys_t, ds))):
                out_t = out_t.astype(jnp.bfloat16)
                out = dot_nt(
                    perm[...], jnp.concatenate([out_t[:, :ROWS], out_t[:, ROWS:]], axis=0)
                )
                send[:, i, :, cols] = out.reshape(N, BLK, 2 * HD).astype(jnp.bfloat16)

        for p in peers:
            placed(g, p).start()
        kept(g).start()

        dv = dot(probs[...], stacked(do_ref, 0, GROUP))
        both = jnp.concatenate([stacked(q_ref, 0, GROUP), ones[...]], axis=1)
        dk = dot(dscore[...], both)
        part[g, :, 0] = dk[: 2 * ROWS, :HD].reshape(2, ROWS, HD).astype(jnp.bfloat16)
        part[g, :, 1] = dv[: 2 * ROWS].reshape(2, ROWS, HD).astype(jnp.bfloat16)
        for slot in (1, 0):

            @pl.when(me >= 2 - slot)
            def _():
                term(g, slot).start()

        own[g, 0] = dk[2 * ROWS :, :HD]
        own[g, 1] = dv[2 * ROWS :]
        colsum[g, 0] = jnp.broadcast_to(jnp.sum(dk[:, :HD], axis=0, keepdims=True), (8, HD))
        colsum[g, 1] = jnp.broadcast_to(jnp.sum(dv, axis=0, keepdims=True), (8, HD))
        high, low = halves(dk[:, HD:])
        query_sum = dot(keys_t, high) + dot(keys_t, low)
        bvec[g] = query_sum.T[:GROUP]

        @pl.when(me != g)
        def _():
            to_owner(g).start()

        return carry

    lax.fori_loop(0, HK, group_step, 0)

    for g in range(HK):
        bvec[HK, g : g + 1] = colsum[g, 0, :1]
        bvec[HK, HK + g : HK + g + 1] = colsum[g, 1, :1]

    @pl.when(me != HK)
    def _():
        to_owner(HK).start()

    def spread(j):
        s = seqs[j]
        return remote(b2.at[0], b2.at[1 + j], p2_s.at[j], p2_r.at[j], {"dp": s})

    def to_all(j, p):
        return remote(btot.at[me], btot.at[me], p3_s.at[j], p3_r.at[me], {"ctx": p})

    @pl.when(me < SLICES)
    def _():
        total = bvec[me]
        for p in peers:
            remote(bvec.at[me], b1.at[p], p1_s.at[me], p1_r.at[p], {"ctx": p}).wait_recv()
        for p in peers:
            total = total + b1[p]
        b2[0] = total
        for j in range(N - 1):
            spread(j).start()
        for j in range(N - 1):
            spread(j).wait_recv()
        rank = [lax.rem(s + N - seq, N) for s in range(N)]
        total = b2[rank[0]]
        for s in range(1, N):
            total = total + b2[rank[s]]
        btot[me] = total
        for j, p in enumerate(peers):
            to_all(j, p).start()

    for s in range(SLICES):

        @pl.when(me != s)
        def _():
            remote(btot.at[s], btot.at[s], p3_s.at[0], p3_r.at[s], {"ctx": s}).wait_recv()

    bias_ref[...] = btot[...]

    for g in range(HK):
        for slot in (1, 0):

            @pl.when(me + (2 - slot) < N)
            def _():
                term(g, slot).wait_recv()

            @pl.when(me + (2 - slot) >= N)
            def _():
                part_in[g, slot] = jnp.zeros((2, ROWS, HD), jnp.bfloat16)

        for i, ref in enumerate((gk_ref, gv_ref)):
            total = own[g, i] + part_in[g, 1, i].astype(jnp.float32)
            total = total + part_in[g, 0, i].astype(jnp.float32)
            ref[:, g * HD : (g + 1) * HD] = total.astype(jnp.bfloat16)

    def finish(g, carry):
        for slot in (1, 0):

            @pl.when(me + (2 - slot) < N)
            def _():
                halo(g, slot).wait_send()

            @pl.when(me >= 2 - slot)
            def _():
                term(g, slot).wait_send()

        @pl.when(me != g)
        def _():
            to_owner(g).wait_send()

        for p in peers:
            placed(g, p).wait_send()
        kept(g).wait()
        for p in peers:
            arrived(g, p).wait_recv()
        return carry

    lax.fori_loop(0, HK, finish, 0)

    @pl.when(me != HK)
    def _():
        to_owner(HK).wait_send()

    @pl.when(me < SLICES)
    def _():
        for j in range(N - 1):
            spread(j).wait_send()
        for j, p in enumerate(peers):
            to_all(j, p).wait_send()


def local(queries, keys, values, grad_out, doc_lengths, placement):
    smem = pl.BlockSpec(memory_space=pltpu.SMEM)
    vmem = pl.BlockSpec(memory_space=pltpu.VMEM)
    bf16, f32 = jnp.bfloat16, jnp.float32
    dma = pltpu.SemaphoreType.DMA
    rows, grad_k, grad_v, bias = pl.pallas_call(
        kernel,
        out_shape=(
            jax.ShapeDtypeStruct((N, 2, BLK, HQ * HD), bf16),
            jax.ShapeDtypeStruct((ROWS, HK * HD), bf16),
            jax.ShapeDtypeStruct((ROWS, HK * HD), bf16),
            jax.ShapeDtypeStruct((SLICES, 8, HD), f32),
        ),
        in_specs=[smem, smem, vmem, vmem, vmem, vmem],
        out_specs=(pl.BlockSpec(memory_space=pl.ANY), vmem, vmem, vmem),
        scratch_shapes=[
            pltpu.VMEM((HK, 3, 2, ROWS, HD), bf16),
            pltpu.VMEM((N, 2, BLK, HQ * HD), bf16),
            pltpu.VMEM((ROWS, ROWS), bf16),
            pltpu.VMEM((WIN, ROWS), f32),
            pltpu.VMEM((WIN, GROUP * ROWS), bf16),
            pltpu.VMEM((WIN, GROUP * ROWS), bf16),
            pltpu.VMEM((GROUP * ROWS, HD), bf16),
            pltpu.VMEM((HK, 2, 2, ROWS, HD), bf16),
            pltpu.VMEM((HK, 2, 2, ROWS, HD), bf16),
            pltpu.VMEM((HK, 2, ROWS, HD), f32),
            pltpu.VMEM((HK, 2, 8, HD), f32),
            pltpu.VMEM((SLICES, 8, HD), f32),
            pltpu.VMEM((N, 8, HD), f32),
            pltpu.VMEM((N, 8, HD), f32),
            pltpu.VMEM((SLICES, 8, HD), f32),
            dma((HK, 2)), dma((HK, 2)),
            dma((HK, N)), dma((HK, N)), dma((HK,)),
            dma((HK, 2)), dma((HK, 2)),
            dma((SLICES,)), dma((N,)),
            dma((N,)), dma((N,)),
            dma((N,)), dma((SLICES,)),
        ],
        compiler_params=pltpu.CompilerParams(
            collective_id=0, has_side_effects=True, vmem_limit_bytes=48 * 1024 * 1024
        ),
        cost_estimate=pl.CostEstimate(
            flops=2 * 6 * ROWS * HQ * HD * WIN,
            bytes_accessed=6 * 1024 * 1024,
            transcendentals=ROWS * HQ * WIN,
        ),
    )(doc_lengths, placement, queries[0], keys[0], values[0], grad_out[0])
    return (
        rows[:, 0].reshape(1, ROWS, HQ * HD),
        rows[:, 1].reshape(1, ROWS, HQ * HD),
        grad_k[None],
        grad_v[None],
        bias.reshape(SLICES * 8 * HD),
    )


def solution(mesh):
    return jax.shard_map(
        local,
        mesh=mesh,
        in_specs=(
            P("dp", "ctx", None),
            P("dp", "ctx", None),
            P("dp", "ctx", None),
            P("dp", "ctx", None),
            P("dp", None),
            P("dp", None, None),
        ),
        out_specs=(
            P("dp", "ctx", None),
            P("dp", "ctx", None),
            P("dp", "ctx", None),
            P("dp", "ctx", None),
            P(),
        ),
        check_vma=False,
    )
```

```python
import contextlib
import math

import jax
import jax.numpy as jnp
from jax import lax
from jax.experimental import pallas as pl
from jax.experimental.pallas import tpu as pltpu
from jax.sharding import PartitionSpec as P

HD = 128
HQ = 32
HK = 4
GROUP = HQ // HK
ROWS = 128
WIN = 384
BLK = 8
N = 16
MESH = pl.DeviceIdType.MESH
NT = (((1,), (1,)), ((), ()))
SCALE = 1.0 / math.sqrt(HD)
LOG2E = math.log2(math.e)
SLICES = HK + 1
FIRST_OWNER = 3
HELD = 2


SCOPES = False


def scope(name):
    return jax.named_scope(name) if SCOPES else contextlib.nullcontext()


def dot(a, b):
    return jnp.dot(a, b, preferred_element_type=jnp.float32)


def dot_nt(a, b):
    return lax.dot_general(a, b, NT, preferred_element_type=jnp.float32)


def halves(x):
    high = x.astype(jnp.bfloat16)
    return high, (x - high.astype(jnp.float32)).astype(jnp.bfloat16)


def kernel(
    len_hbm, place_hbm, q_hbm, k_hbm, v_hbm, do_hbm,
    rows_ref, bias_ref,
    len_ref, place_ref, q_ref, k_ref, v_ref, do_ref, in_s, gkv, gkv_s, win, win_relay, send, perm, mask,
    probs, dscore, ones, part, part_in, part_relay, own, colsum, bvec, b1, b2, b3, btot,
    halo_s, halo_r, relay_s, relay_r, back_s, back_r, a2a_s, a2a_r, loc_s, part_s, part_r,
    p1_s, p1_r, p2_s, p2_r, p3_s, p3_r, p4_s, p4_r,
):
    me = lax.axis_index("ctx")
    seq = lax.axis_index("dp")
    half = me // 8
    inner = lax.rem(me, 8)

    x = seq // 4
    low = lax.rem(seq, 4)
    depth = half * 4 + low
    core = lax.rem(me, 2)

    across = [(1 - half) * 8 + lax.rem(inner + j, 8) for j in range(8)]
    near = [half * 8 + lax.rem(inner + j, 8) for j in range(1, 8)]
    peers = [{"ctx": p} for p in across + near]
    along_x = [{"dp": lax.rem(x + j, 4) * 4 + low} for j in range(1, 4)]
    along_z = []
    for j in range(1, 8):
        z = lax.rem(depth + j, 8)
        along_z.append({"ctx": (z // 4) * 8 + inner, "dp": x * 4 + lax.rem(z, 4)})
    others = peers + along_x + [along_z[j - 1] for j in range(1, 8) if j != 4]

    def remote(src, dst, send_sem, recv_sem, device):
        return pltpu.make_async_remote_copy(
            src_ref=src, dst_ref=dst, send_sem=send_sem, recv_sem=recv_sem,
            device_id=device, device_id_type=MESH,
        )

    def columns(g):
        return pl.ds(pl.multiple_of(g * GROUP * HD, GROUP * HD), GROUP * HD)

    def fetch_q(g):
        return pltpu.make_async_copy(q_hbm.at[:, columns(g)], q_ref.at[:, columns(g)], in_s.at[g])

    def fetch_do(g):
        return pltpu.make_async_copy(
            do_hbm.at[:, columns(g)], do_ref.at[:, columns(g)], in_s.at[HK + g]
        )

    small = [
        pltpu.make_async_copy(src, dst, in_s.at[2 * HK + i])
        for i, (src, dst) in enumerate(
            ((k_hbm, k_ref), (v_hbm, v_ref), (len_hbm, len_ref), (place_hbm, place_ref))
        )
    ]
    with scope("signals"):
        for copy in small:
            copy.start()
        barrier = pltpu.get_barrier_semaphore()
        for device in others:
            pl.semaphore_signal(barrier, inc=1, device_id=device, device_id_type=MESH)
        for g in range(HK):
            fetch_q(g).start()
            fetch_do(g).start()
        for copy in small:
            copy.wait()

    for g in range(HK):
        win[g, 2, 0] = k_ref[:, g * HD : (g + 1) * HD]
        win[g, 2, 1] = v_ref[:, g * HD : (g + 1) * HD]

    @pl.when(me < 2)
    def _():
        win[:, 0] = jnp.zeros((HK, 2, ROWS, HD), jnp.bfloat16)

    @pl.when(me < 1)
    def _():
        win[:, 1] = jnp.zeros((HK, 2, ROWS, HD), jnp.bfloat16)

    lane = lax.broadcasted_iota(jnp.int32, (1, ROWS), 1)
    pos = me * ROWS + lane
    first = jnp.zeros((1, ROWS), jnp.int32)
    start = len_ref[0, 0] * 0
    for i in range(N):
        first = jnp.where(pos >= start, start, first)
        start = start + len_ref[0, i]
    t_pos = (me - 2) * ROWS + lax.broadcasted_iota(jnp.int32, (WIN, ROWS), 0)
    seen = (t_pos >= first) & (t_pos <= pos)
    mask[...] = jnp.where(seen, 0.0, -1e30)

    target = lax.rem(lane, BLK)
    for j in range(N):
        target = target + jnp.where(lane // BLK == j, place_ref[0, me, j] * BLK, 0)
    row = lax.broadcasted_iota(jnp.int32, (ROWS, ROWS), 0)
    perm[...] = jnp.where(row == target, 1.0, 0.0).astype(jnp.bfloat16)
    ones[...] = jnp.where(
        lax.broadcasted_iota(jnp.int32, (GROUP * ROWS, HD), 0) // ROWS
        == lax.broadcasted_iota(jnp.int32, (GROUP * ROWS, HD), 1),
        1.0, 0.0,
    ).astype(jnp.bfloat16)

    with scope("barrier"):
        pl.semaphore_wait(barrier, len(others))

    def halo(g, slot):
        return remote(
            win.at[g, 2], win.at[g, slot], halo_s.at[g, slot], halo_r.at[g, slot],
            {"ctx": lax.rem(me + (2 - slot), N)},
        )

    def term(g, slot):
        return remote(
            part.at[g, slot], part_in.at[g, slot], part_s.at[g, slot], part_r.at[g, slot],
            {"ctx": lax.rem(me + N - (2 - slot), N)},
        )

    column = inner // 2
    relay_head = HK - 1 - column

    def leaves(slot):
        return (half == 0) & (me + (2 - slot) >= 8)

    def returns(slot):
        return (half == 1) & (me - (2 - slot) < 8)

    def has_next(g, slot):
        return (me + (2 - slot) < N) & (jnp.logical_not(leaves(slot)) | (g == 0))

    def to_relay(g):
        return remote(
            win.at[g, 2], win_relay, halo_s.at[g, 0], relay_r.at[0],
            {"ctx": 2 * (HK - 1 - g) + core},
        )

    def relayed(slot):
        return remote(
            win_relay, win.at[relay_head, slot], relay_s.at[slot], halo_r.at[relay_head, slot],
            {"ctx": 6 + core + (2 - slot)},
        )

    is_relay = (half == 0) & (column < HK - 1)

    with scope("halo_start"):
        for g in range(HK):
            for slot in (1, 0):

                @pl.when(has_next(g, slot))
                def _():
                    halo(g, slot).start()

            if g > 0:

                @pl.when((half == 0) & (column == HK - 1))
                def _():
                    to_relay(g).start()

        @pl.when(is_relay)
        def _():
            to_relay(1).wait_recv()
            relayed(0).start()

            @pl.when(core == 1)
            def _():
                relayed(1).start()

    def has_before(g, slot):
        return (me >= 2 - slot) & (jnp.logical_not(returns(slot)) | (g == HK - 1))

    def term_to_relay(g, slot):
        return remote(
            part.at[g, slot], part_relay.at[slot], part_s.at[g, slot], back_r.at[slot],
            {"ctx": 8 + 2 * (HK - 1 - g) + core},
        )

    def term_relayed(slot):
        return remote(
            part_relay.at[slot], part_in.at[relay_head, slot], back_s.at[slot],
            part_r.at[relay_head, slot], {"ctx": 8 + core - (2 - slot)},
        )

    is_back_relay = (half == 1) & (column > 0)

    def placed(g, p):
        cols = columns(g)
        return remote(
            send.at[p, :, :, cols], rows_ref.at[me, :, :, cols], a2a_s.at[g, p], a2a_r.at[g, me],
            {"ctx": p},
        )

    def arrived(g, p):
        cols = columns(g)
        return remote(
            send.at[p, :, :, cols], rows_ref.at[p, :, :, cols], a2a_s.at[g, p], a2a_r.at[g, p],
            {"ctx": p},
        )

    def kept(g):
        cols = columns(g)
        return pltpu.make_async_copy(
            send.at[me, :, :, cols], rows_ref.at[me, :, :, cols], loc_s.at[g]
        )

    def to_owner(s):
        return remote(
            bvec.at[s], b1.at[inner], p1_s.at[s], p1_r.at[inner],
            {"ctx": half * 8 + s + FIRST_OWNER},
        )

    is_owner = inner >= FIRST_OWNER

    def group_step(g, carry):
        with scope("halo"):
            fetch_q(g).wait()
            fetch_do(g).wait()
            for slot in (1, 0):

                @pl.when(me >= 2 - slot)
                def _():
                    halo(g, slot).wait_recv()

        keys = win[g, :, 0].reshape(WIN, HD)
        values = win[g, :, 1].reshape(WIN, HD)
        keys_t = keys.astype(jnp.float32).T.astype(jnp.bfloat16)
        values_t = values.astype(jnp.float32).T.astype(jnp.bfloat16)
        shut = jnp.concatenate([mask[...], mask[...]], axis=1)

        def stacked(ref, first_head, count):
            cols = pl.ds(pl.multiple_of((g * GROUP + first_head) * HD, HD), count * HD)
            x = ref[:, cols]
            return jnp.concatenate([x[:, i * HD : (i + 1) * HD] for i in range(count)], axis=0)

        with scope("heads"):
            for pair in range(GROUP // 2):
                q2 = stacked(q_ref, pair * 2, 2)
                do2 = stacked(do_ref, pair * 2, 2)
                scores = dot_nt(keys, q2) + shut
                top = jnp.max(scores, axis=0, keepdims=True)
                e = jnp.exp2((scores - top) * (SCALE * LOG2E))
                inv = 1.0 / jnp.sum(e, axis=0, keepdims=True)
                weights = (e * inv).astype(jnp.bfloat16)
                grad = dot_nt(values, do2)
                delta = jnp.sum(weights.astype(jnp.float32) * grad, axis=0, keepdims=True)
                ds = (e * (inv * SCALE) * (grad - delta)).astype(jnp.bfloat16)
                at = slice(pair * 2 * ROWS, (pair + 1) * 2 * ROWS)
                probs[:, at] = weights
                dscore[:, at] = ds
                cols = pl.ds(pl.multiple_of((g * GROUP + pair * 2) * HD, 2 * HD), 2 * HD)
                for i, out_t in enumerate((dot(values_t, weights), dot(keys_t, ds))):
                    out_t = out_t.astype(jnp.bfloat16)
                    out = dot_nt(
                        perm[...], jnp.concatenate([out_t[:, :ROWS], out_t[:, ROWS:]], axis=0)
                    )
                    send[:, i, :, cols] = out.reshape(N, BLK, 2 * HD).astype(jnp.bfloat16)

        with scope("sends"):

            @pl.when((g < HELD) | jnp.logical_not(is_owner))
            def _():
                for p in across:
                    placed(g, p).start()

            for p in near:
                placed(g, p).start()
            kept(g).start()

        with scope("terms"):
            dv = dot(probs[...], stacked(do_ref, 0, GROUP))
            both = jnp.concatenate([stacked(q_ref, 0, GROUP), ones[...]], axis=1)
            dk = dot(dscore[...], both)
            part[g, :, 0] = dk[: 2 * ROWS, :HD].reshape(2, ROWS, HD).astype(jnp.bfloat16)
            part[g, :, 1] = dv[: 2 * ROWS].reshape(2, ROWS, HD).astype(jnp.bfloat16)
            for slot in (1, 0):

                @pl.when(has_before(g, slot))
                def _():
                    term(g, slot).start()

                @pl.when(returns(slot) & (g < HK - 1))
                def _():
                    term_to_relay(g, slot).start()

            own[g, 0] = dk[2 * ROWS :, :HD]
            own[g, 1] = dv[2 * ROWS :]
            colsum[g, 0] = jnp.broadcast_to(jnp.sum(dk[:, :HD], axis=0, keepdims=True), (8, HD))
            colsum[g, 1] = jnp.broadcast_to(jnp.sum(dv, axis=0, keepdims=True), (8, HD))
            high, low = halves(dk[:, HD:])
            query_sum = dot(keys_t, high) + dot(keys_t, low)
            bvec[g] = query_sum.T[:GROUP]

            @pl.when(inner != g + FIRST_OWNER)
            def _():
                to_owner(g).start()

        return carry

    lax.fori_loop(0, HK, group_step, 0)

    for g in range(HK):
        bvec[HK, g : g + 1] = colsum[g, 0, :1]
        bvec[HK, HK + g : HK + g + 1] = colsum[g, 1, :1]

    @pl.when(inner != HK + FIRST_OWNER)
    def _():
        to_owner(HK).start()

    mine = inner - FIRST_OWNER

    def to_x(j):
        return remote(b2.at[x], b2.at[x], p2_s.at[j], p2_r.at[x], along_x[j - 1])

    def from_x(j):
        at = lax.rem(x + j, 4)
        return remote(b2.at[at], b2.at[at], p2_s.at[j], p2_r.at[at], along_x[j - 1])

    def to_z(j):
        return remote(b3.at[depth], b3.at[depth], p3_s.at[j], p3_r.at[depth], along_z[j - 1])

    def from_z(j):
        at = lax.rem(depth + j, 8)
        return remote(b3.at[at], b3.at[at], p3_s.at[j], p3_r.at[at], along_z[j - 1])

    def to_near(j):
        device = {"ctx": near[j - 1]}
        return remote(btot.at[mine], btot.at[mine], p4_s.at[j], p4_r.at[mine], device)

    with scope("owner"):

        @pl.when(is_owner)
        def _():
            b1[inner] = bvec[mine]
            for j in range(1, 8):
                at = lax.rem(inner + j, 8)
                remote(
                    bvec.at[mine], b1.at[at], p1_s.at[mine], p1_r.at[at], {"ctx": near[j - 1]}
                ).wait_recv()
            total = b1[0]
            for j in range(1, 8):
                total = total + b1[j]
            b2[x] = total
            for j in range(1, 4):
                to_x(j).start()
            for j in range(1, 4):
                from_x(j).wait_recv()
            b3[depth] = (b2[0] + b2[1]) + (b2[2] + b2[3])
            for j in range(1, 8):
                to_z(j).start()
            for g in range(HELD, HK):
                for p in across:
                    placed(g, p).start()
            for j in range(1, 8):
                from_z(j).wait_recv()
            total = b3[0]
            for j in range(1, 8):
                total = total + b3[j]
            btot[mine] = total
            for j in range(1, 8):
                to_near(j).start()

    with scope("relay"):

        @pl.when(is_back_relay)
        def _():
            term_to_relay(0, 0).wait_recv()
            term_relayed(0).start()

            @pl.when(core == 0)
            def _():
                term_to_relay(0, 1).wait_recv()
                term_relayed(1).start()

    with scope("bias"):
        for s in range(SLICES):

            @pl.when(inner != s + FIRST_OWNER)
            def _():
                remote(
                    btot.at[s], btot.at[s], p4_s.at[0], p4_r.at[s],
                    {"ctx": half * 8 + s + FIRST_OWNER},
                ).wait_recv()

    bias_ref[...] = btot[...]

    with scope("gkv"):
        for g in range(HK):
            for slot in (1, 0):

                @pl.when(me + (2 - slot) < N)
                def _():
                    term(g, slot).wait_recv()

                @pl.when(me + (2 - slot) >= N)
                def _():
                    part_in[g, slot] = jnp.zeros((2, ROWS, HD), jnp.bfloat16)

            for i in range(2):
                total = own[g, i] + part_in[g, 1, i].astype(jnp.float32)
                total = total + part_in[g, 0, i].astype(jnp.float32)
                gkv[:, i, :, g * HD : (g + 1) * HD] = total.reshape(N, BLK, HD).astype(
                    jnp.bfloat16
                )
        result = pltpu.make_async_copy(gkv, rows_ref.at[:, :, :, HQ * HD :], gkv_s)
        result.start()

    def finish(g, carry):
        for slot in (1, 0):

            @pl.when(has_next(g, slot))
            def _():
                halo(g, slot).wait_send()

            @pl.when(has_before(g, slot))
            def _():
                term(g, slot).wait_send()

            @pl.when(returns(slot) & (g < HK - 1))
            def _():
                term_to_relay(g, slot).wait_send()

        @pl.when((half == 0) & (column == HK - 1) & (g > 0))
        def _():
            to_relay(g).wait_send()

        @pl.when(inner != g + FIRST_OWNER)
        def _():
            to_owner(g).wait_send()

        for p in across + near:
            placed(g, p).wait_send()
        kept(g).wait()
        for p in near + across:
            arrived(g, p).wait_recv()
        return carry

    with scope("finish"):
        lax.fori_loop(0, HK, finish, 0)
        result.wait()

    @pl.when(inner != HK + FIRST_OWNER)
    def _():
        to_owner(HK).wait_send()

    @pl.when(is_relay)
    def _():
        relayed(0).wait_send()

        @pl.when(core == 1)
        def _():
            relayed(1).wait_send()

    @pl.when(is_back_relay)
    def _():
        term_relayed(0).wait_send()

        @pl.when(core == 0)
        def _():
            term_relayed(1).wait_send()

    @pl.when(is_owner)
    def _():
        for j in range(1, 4):
            to_x(j).wait_send()
        for j in range(1, 8):
            to_z(j).wait_send()
            to_near(j).wait_send()


def local(queries, keys, values, grad_out, doc_lengths, placement):
    vmem = pl.BlockSpec(memory_space=pltpu.VMEM)
    bf16, f32 = jnp.bfloat16, jnp.float32
    dma = pltpu.SemaphoreType.DMA
    rows, bias = pl.pallas_call(
        kernel,
        out_shape=(
            jax.ShapeDtypeStruct((N, 2, BLK, (HQ + HK) * HD), bf16),
            jax.ShapeDtypeStruct((SLICES, 8, HD), f32),
        ),
        in_specs=[pl.BlockSpec(memory_space=pltpu.HBM)] * 6,
        out_specs=(pl.BlockSpec(memory_space=pl.ANY), vmem),
        scratch_shapes=[
            pltpu.SMEM((1, N), jnp.int32),
            pltpu.SMEM((1, N, N), jnp.int32),
            pltpu.VMEM((ROWS, HQ * HD), bf16),
            pltpu.VMEM((ROWS, HK * HD), bf16),
            pltpu.VMEM((ROWS, HK * HD), bf16),
            pltpu.VMEM((ROWS, HQ * HD), bf16),
            dma((2 * HK + 4,)),
            pltpu.VMEM((N, 2, BLK, HK * HD), bf16),
            dma,
            pltpu.VMEM((HK, 3, 2, ROWS, HD), bf16),
            pltpu.VMEM((2, ROWS, HD), bf16),
            pltpu.VMEM((N, 2, BLK, HQ * HD), bf16),
            pltpu.VMEM((ROWS, ROWS), bf16),
            pltpu.VMEM((WIN, ROWS), f32),
            pltpu.VMEM((WIN, GROUP * ROWS), bf16),
            pltpu.VMEM((WIN, GROUP * ROWS), bf16),
            pltpu.VMEM((GROUP * ROWS, HD), bf16),
            pltpu.VMEM((HK, 2, 2, ROWS, HD), bf16),
            pltpu.VMEM((HK, 2, 2, ROWS, HD), bf16),
            pltpu.VMEM((2, 2, ROWS, HD), bf16),
            pltpu.VMEM((HK, 2, ROWS, HD), f32),
            pltpu.VMEM((HK, 2, 8, HD), f32),
            pltpu.VMEM((SLICES, 8, HD), f32),
            pltpu.VMEM((8, 8, HD), f32),
            pltpu.VMEM((4, 8, HD), f32),
            pltpu.VMEM((8, 8, HD), f32),
            pltpu.VMEM((SLICES, 8, HD), f32),
            dma((HK, 2)), dma((HK, 2)), dma((2,)), dma((1,)), dma((2,)), dma((2,)),
            dma((HK, N)), dma((HK, N)), dma((HK,)),
            dma((HK, 2)), dma((HK, 2)),
            dma((SLICES,)), dma((8,)), dma((4,)), dma((4,)),
            dma((8,)), dma((8,)), dma((8,)), dma((SLICES,)),
        ],
        compiler_params=pltpu.CompilerParams(
            collective_id=0, has_side_effects=True, vmem_limit_bytes=60 * 1024 * 1024
        ),
        cost_estimate=pl.CostEstimate(
            flops=2 * 6 * ROWS * HQ * HD * WIN,
            bytes_accessed=6 * 1024 * 1024,
            transcendentals=ROWS * HQ * WIN,
        ),
    )(doc_lengths, placement, queries[0], keys[0], values[0], grad_out[0])
    return (
        rows[:, 0, :, : HQ * HD].reshape(1, ROWS, HQ * HD),
        rows[:, 1, :, : HQ * HD].reshape(1, ROWS, HQ * HD),
        rows[:, 0, :, HQ * HD :].reshape(1, ROWS, HK * HD),
        rows[:, 1, :, HQ * HD :].reshape(1, ROWS, HK * HD),
        bias.reshape(SLICES * 8 * HD),
    )


def solution(mesh):
    return jax.shard_map(
        local,
        mesh=mesh,
        in_specs=(
            P("dp", "ctx", None),
            P("dp", "ctx", None),
            P("dp", "ctx", None),
            P("dp", "ctx", None),
            P("dp", None),
            P("dp", None, None),
        ),
        out_specs=(
            P("dp", "ctx", None),
            P("dp", "ctx", None),
            P("dp", "ctx", None),
            P("dp", "ctx", None),
            P(),
        ),
        check_vma=False,
    )
```

```python
import contextlib
import math

import jax
import jax.numpy as jnp
from jax import lax
from jax.experimental import pallas as pl
from jax.experimental.pallas import tpu as pltpu
from jax.sharding import PartitionSpec as P

HD = 128
HQ = 32
HK = 4
GROUP = HQ // HK
ROWS = 128
WIN = 384
BLK = 8
N = 16
MESH = pl.DeviceIdType.MESH
NT = (((1,), (1,)), ((), ()))
SCALE = 1.0 / math.sqrt(HD)
LOG2E = math.log2(math.e)
SLICES = HK + 1
FIRST_OWNER = 3
HELD = 3
EARLY = 2 * HD


SCOPES = False


def scope(name):
    return jax.named_scope(name) if SCOPES else contextlib.nullcontext()


def dot(a, b):
    return jnp.dot(a, b, preferred_element_type=jnp.float32)


def dot_nt(a, b):
    return lax.dot_general(a, b, NT, preferred_element_type=jnp.float32)


def halves(x):
    high = x.astype(jnp.bfloat16)
    return high, (x - high.astype(jnp.float32)).astype(jnp.bfloat16)


def kernel(
    len_hbm, place_hbm, q_hbm, k_hbm, v_hbm, do_hbm,
    rows_ref, bias_ref,
    len_ref, place_ref, q_ref, k_ref, v_ref, do_ref, in_s, gkv, gkv_s, win, win_relay, send, perm, mask,
    probs, dscore, ones, part, part_in, part_relay, own, colsum, bvec, b1, b2, b3, btot,
    halo_s, halo_r, relay_s, relay_r, back_s, back_r, a2a_s, a2a_r, loc_s, part_s, part_r,
    p1_s, p1_r, p2_s, p2_r, p3_s, p3_r, p4_s, p4_r,
):
    me = lax.axis_index("ctx")
    seq = lax.axis_index("dp")
    half = me // 8
    inner = lax.rem(me, 8)

    x = seq // 4
    low = lax.rem(seq, 4)
    depth = half * 4 + low
    core = lax.rem(me, 2)

    across = [(1 - half) * 8 + lax.rem(inner + j, 8) for j in range(8)]
    near = [half * 8 + lax.rem(inner + j, 8) for j in range(1, 8)]
    peers = [{"ctx": p} for p in across + near]
    along_x = [{"dp": lax.rem(x + j, 4) * 4 + low} for j in range(1, 4)]
    along_z = []
    for j in range(1, 8):
        z = lax.rem(depth + j, 8)
        along_z.append({"ctx": (z // 4) * 8 + inner, "dp": x * 4 + lax.rem(z, 4)})
    others = peers + along_x + [along_z[j - 1] for j in range(1, 8) if j != 4]

    def remote(src, dst, send_sem, recv_sem, device):
        return pltpu.make_async_remote_copy(
            src_ref=src, dst_ref=dst, send_sem=send_sem, recv_sem=recv_sem,
            device_id=device, device_id_type=MESH,
        )

    def columns(g):
        return pl.ds(pl.multiple_of(g * GROUP * HD, GROUP * HD), GROUP * HD)

    def fetch_q(g):
        return pltpu.make_async_copy(q_hbm.at[:, columns(g)], q_ref.at[:, columns(g)], in_s.at[g])

    def fetch_do(g):
        return pltpu.make_async_copy(
            do_hbm.at[:, columns(g)], do_ref.at[:, columns(g)], in_s.at[HK + g]
        )

    small = [
        pltpu.make_async_copy(src, dst, in_s.at[2 * HK + i])
        for i, (src, dst) in enumerate(
            ((k_hbm, k_ref), (v_hbm, v_ref), (len_hbm, len_ref), (place_hbm, place_ref))
        )
    ]
    with scope("signals"):
        for copy in small:
            copy.start()
        barrier = pltpu.get_barrier_semaphore()
        for device in others:
            pl.semaphore_signal(barrier, inc=1, device_id=device, device_id_type=MESH)
        for g in range(HK):
            fetch_q(g).start()
            fetch_do(g).start()
        for copy in small:
            copy.wait()

    for g in range(HK):
        win[g, 2, 0] = k_ref[:, g * HD : (g + 1) * HD]
        win[g, 2, 1] = v_ref[:, g * HD : (g + 1) * HD]

    @pl.when(me < 2)
    def _():
        win[:, 0] = jnp.zeros((HK, 2, ROWS, HD), jnp.bfloat16)

    @pl.when(me < 1)
    def _():
        win[:, 1] = jnp.zeros((HK, 2, ROWS, HD), jnp.bfloat16)

    with scope("barrier"):
        pl.semaphore_wait(barrier, len(others))

    def halo(g, slot):
        return remote(
            win.at[g, 2], win.at[g, slot], halo_s.at[g, slot], halo_r.at[g, slot],
            {"ctx": lax.rem(me + (2 - slot), N)},
        )

    def term(g, slot):
        return remote(
            part.at[g, slot], part_in.at[g, slot], part_s.at[g, slot], part_r.at[g, slot],
            {"ctx": lax.rem(me + N - (2 - slot), N)},
        )

    column = inner // 2
    relay_head = HK - 1 - column

    def leaves(slot):
        return (half == 0) & (me + (2 - slot) >= 8)

    def returns(slot):
        return (half == 1) & (me - (2 - slot) < 8)

    def has_next(g, slot):
        return (me + (2 - slot) < N) & (jnp.logical_not(leaves(slot)) | (g == 0))

    def to_relay(g):
        return remote(
            win.at[g, 2], win_relay, halo_s.at[g, 0], relay_r.at[0],
            {"ctx": 2 * (HK - 1 - g) + core},
        )

    def relayed(slot):
        return remote(
            win_relay, win.at[relay_head, slot], relay_s.at[slot], halo_r.at[relay_head, slot],
            {"ctx": 6 + core + (2 - slot)},
        )

    is_relay = (half == 0) & (column < HK - 1)

    with scope("halo_start"):
        for g in range(HK):
            for slot in (1, 0):

                @pl.when(has_next(g, slot))
                def _():
                    halo(g, slot).start()

            if g > 0:

                @pl.when((half == 0) & (column == HK - 1))
                def _():
                    to_relay(g).start()

        @pl.when(is_relay)
        def _():
            to_relay(1).wait_recv()
            relayed(0).start()

            @pl.when(core == 1)
            def _():
                relayed(1).start()

    lane = lax.broadcasted_iota(jnp.int32, (1, ROWS), 1)
    pos = me * ROWS + lane
    first = jnp.zeros((1, ROWS), jnp.int32)
    start = len_ref[0, 0] * 0
    for i in range(N):
        first = jnp.where(pos >= start, start, first)
        start = start + len_ref[0, i]
    t_pos = (me - 2) * ROWS + lax.broadcasted_iota(jnp.int32, (WIN, ROWS), 0)
    seen = (t_pos >= first) & (t_pos <= pos)
    mask[...] = jnp.where(seen, 0.0, -1e30)

    target = lax.rem(lane, BLK)
    for j in range(N):
        target = target + jnp.where(lane // BLK == j, place_ref[0, me, j] * BLK, 0)
    row = lax.broadcasted_iota(jnp.int32, (ROWS, ROWS), 0)
    perm[...] = jnp.where(row == target, 1.0, 0.0).astype(jnp.bfloat16)
    ones[...] = jnp.where(
        lax.broadcasted_iota(jnp.int32, (GROUP * ROWS, HD), 0) // ROWS
        == lax.broadcasted_iota(jnp.int32, (GROUP * ROWS, HD), 1),
        1.0, 0.0,
    ).astype(jnp.bfloat16)

    def has_before(g, slot):
        return (me >= 2 - slot) & (jnp.logical_not(returns(slot)) | (g == HK - 1))

    def term_to_relay(g, slot):
        return remote(
            part.at[g, slot], part_relay.at[slot], part_s.at[g, slot], back_r.at[slot],
            {"ctx": 8 + 2 * (HK - 1 - g) + core},
        )

    def term_relayed(slot):
        return remote(
            part_relay.at[slot], part_in.at[relay_head, slot], back_s.at[slot],
            part_r.at[relay_head, slot], {"ctx": 8 + core - (2 - slot)},
        )

    is_back_relay = (half == 1) & (column > 0)

    def placed(g, p):
        cols = columns(g)
        return remote(
            send.at[p, :, :, cols], rows_ref.at[me, :, :, cols], a2a_s.at[g, p], a2a_r.at[g, me],
            {"ctx": p},
        )

    def arrived(g, p):
        cols = columns(g)
        return remote(
            send.at[p, :, :, cols], rows_ref.at[p, :, :, cols], a2a_s.at[g, p], a2a_r.at[g, p],
            {"ctx": p},
        )

    def early(part, p, source):
        cols = (slice(0, EARLY), slice(EARLY, GROUP * HD))[part]
        i = (HK, 0)[part]
        return remote(
            send.at[p, :, :, cols], rows_ref.at[source, :, :, cols], a2a_s.at[i, p],
            a2a_r.at[i, source], {"ctx": p},
        )

    def kept(g):
        cols = columns(g)
        return pltpu.make_async_copy(
            send.at[me, :, :, cols], rows_ref.at[me, :, :, cols], loc_s.at[g]
        )

    def to_owner(s):
        return remote(
            bvec.at[s], b1.at[inner], p1_s.at[s], p1_r.at[inner],
            {"ctx": half * 8 + s + FIRST_OWNER},
        )

    is_owner = inner >= FIRST_OWNER
    is_held = inner >= 2

    def group_step(g, carry):
        with scope("halo"):
            fetch_q(g).wait()
            fetch_do(g).wait()
            for slot in (1, 0):

                @pl.when(me >= 2 - slot)
                def _():
                    halo(g, slot).wait_recv()

        keys = win[g, :, 0].reshape(WIN, HD)
        values = win[g, :, 1].reshape(WIN, HD)
        keys_t = keys.astype(jnp.float32).T.astype(jnp.bfloat16)
        values_t = values.astype(jnp.float32).T.astype(jnp.bfloat16)
        shut = jnp.concatenate([mask[...], mask[...]], axis=1)

        def stacked(ref, first_head, count):
            cols = pl.ds(pl.multiple_of((g * GROUP + first_head) * HD, HD), count * HD)
            x = ref[:, cols]
            return jnp.concatenate([x[:, i * HD : (i + 1) * HD] for i in range(count)], axis=0)

        with scope("heads"):
            for pair in range(GROUP // 2):
                q2 = stacked(q_ref, pair * 2, 2)
                do2 = stacked(do_ref, pair * 2, 2)
                scores = dot_nt(keys, q2) + shut
                top = jnp.max(scores, axis=0, keepdims=True)
                e = jnp.exp2((scores - top) * (SCALE * LOG2E))
                inv = 1.0 / jnp.sum(e, axis=0, keepdims=True)
                weights = (e * inv).astype(jnp.bfloat16)
                grad = dot_nt(values, do2)
                delta = jnp.sum(weights.astype(jnp.float32) * grad, axis=0, keepdims=True)
                ds = (e * (inv * SCALE) * (grad - delta)).astype(jnp.bfloat16)
                at = slice(pair * 2 * ROWS, (pair + 1) * 2 * ROWS)
                probs[:, at] = weights
                dscore[:, at] = ds
                cols = pl.ds(pl.multiple_of((g * GROUP + pair * 2) * HD, 2 * HD), 2 * HD)
                for i, out_t in enumerate((dot(values_t, weights), dot(keys_t, ds))):
                    out_t = out_t.astype(jnp.bfloat16)
                    out = dot_nt(
                        perm[...], jnp.concatenate([out_t[:, :ROWS], out_t[:, ROWS:]], axis=0)
                    )
                    send[:, i, :, cols] = out.reshape(N, BLK, 2 * HD).astype(jnp.bfloat16)

                if (pair + 1) * 2 * HD == EARLY:

                    @pl.when(g == 0)
                    def _():
                        for p in across:
                            early(0, p, me).start()

        with scope("sends"):

            @pl.when(g == 0)
            def _():
                for p in across:
                    early(1, p, me).start()

            for p in near:
                placed(g, p).start()
            kept(g).start()

        with scope("terms"):
            dv = dot(probs[...], stacked(do_ref, 0, GROUP))
            both = jnp.concatenate([stacked(q_ref, 0, GROUP), ones[...]], axis=1)
            dk = dot(dscore[...], both)
            part[g, :, 0] = dk[: 2 * ROWS, :HD].reshape(2, ROWS, HD).astype(jnp.bfloat16)
            part[g, :, 1] = dv[: 2 * ROWS].reshape(2, ROWS, HD).astype(jnp.bfloat16)
            for slot in (1, 0):

                @pl.when(has_before(g, slot))
                def _():
                    term(g, slot).start()

                @pl.when(returns(slot) & (g < HK - 1))
                def _():
                    term_to_relay(g, slot).start()

            own[g, 0] = dk[2 * ROWS :, :HD]
            own[g, 1] = dv[2 * ROWS :]
            colsum[g, 0] = jnp.broadcast_to(jnp.sum(dk[:, :HD], axis=0, keepdims=True), (8, HD))
            colsum[g, 1] = jnp.broadcast_to(jnp.sum(dv, axis=0, keepdims=True), (8, HD))
            high, low = halves(dk[:, HD:])
            query_sum = dot(keys_t, high) + dot(keys_t, low)
            bvec[g] = query_sum.T[:GROUP]

            @pl.when(inner != g + FIRST_OWNER)
            def _():
                to_owner(g).start()

        @pl.when((g > 0) & ((g < HELD) | jnp.logical_not(is_held)))
        def _():
            for p in across:
                placed(g, p).start()

        return carry

    lax.fori_loop(0, HK, group_step, 0)

    for g in range(HK):
        bvec[HK, g : g + 1] = colsum[g, 0, :1]
        bvec[HK, HK + g : HK + g + 1] = colsum[g, 1, :1]

    @pl.when(inner != HK + FIRST_OWNER)
    def _():
        to_owner(HK).start()

    mine = inner - FIRST_OWNER

    def to_x(j):
        return remote(b2.at[x], b2.at[x], p2_s.at[j], p2_r.at[x], along_x[j - 1])

    def from_x(j):
        at = lax.rem(x + j, 4)
        return remote(b2.at[at], b2.at[at], p2_s.at[j], p2_r.at[at], along_x[j - 1])

    def to_z(j):
        return remote(b3.at[depth], b3.at[depth], p3_s.at[j], p3_r.at[depth], along_z[j - 1])

    def from_z(j):
        at = lax.rem(depth + j, 8)
        return remote(b3.at[at], b3.at[at], p3_s.at[j], p3_r.at[at], along_z[j - 1])

    def to_near(j):
        device = {"ctx": near[j - 1]}
        return remote(btot.at[mine], btot.at[mine], p4_s.at[j], p4_r.at[mine], device)

    with scope("owner"):

        @pl.when(is_owner)
        def _():
            b1[inner] = bvec[mine]
            for j in range(1, 8):
                at = lax.rem(inner + j, 8)
                remote(
                    bvec.at[mine], b1.at[at], p1_s.at[mine], p1_r.at[at], {"ctx": near[j - 1]}
                ).wait_recv()
            total = b1[0]
            for j in range(1, 8):
                total = total + b1[j]
            b2[x] = total
            for j in range(1, 4):
                to_x(j).start()
            for j in range(1, 4):
                from_x(j).wait_recv()
            b3[depth] = (b2[0] + b2[1]) + (b2[2] + b2[3])
            for j in range(1, 8):
                to_z(j).start()

    with scope("relay"):

        @pl.when(is_back_relay)
        def _():
            term_to_relay(0, 0).wait_recv()
            term_relayed(0).start()

            @pl.when(core == 0)
            def _():
                term_to_relay(0, 1).wait_recv()
                term_relayed(1).start()

    @pl.when(is_held)
    def _():
        for g in range(HELD, HK):
            for p in across:
                placed(g, p).start()

    with scope("total"):

        @pl.when(is_owner)
        def _():
            for j in range(1, 8):
                from_z(j).wait_recv()
            total = b3[0]
            for j in range(1, 8):
                total = total + b3[j]
            btot[mine] = total
            for j in range(1, 8):
                to_near(j).start()

    with scope("bias"):
        for s in range(SLICES):

            @pl.when(inner != s + FIRST_OWNER)
            def _():
                remote(
                    btot.at[s], btot.at[s], p4_s.at[0], p4_r.at[s],
                    {"ctx": half * 8 + s + FIRST_OWNER},
                ).wait_recv()

    bias_ref[...] = btot[...]

    with scope("gkv"):
        for g in range(HK):
            for slot in (1, 0):

                @pl.when(me + (2 - slot) < N)
                def _():
                    term(g, slot).wait_recv()

                @pl.when(me + (2 - slot) >= N)
                def _():
                    part_in[g, slot] = jnp.zeros((2, ROWS, HD), jnp.bfloat16)

            for i in range(2):
                total = own[g, i] + part_in[g, 1, i].astype(jnp.float32)
                total = total + part_in[g, 0, i].astype(jnp.float32)
                gkv[:, i, :, g * HD : (g + 1) * HD] = total.reshape(N, BLK, HD).astype(
                    jnp.bfloat16
                )
        result = pltpu.make_async_copy(gkv, rows_ref.at[:, :, :, HQ * HD :], gkv_s)
        result.start()

    def finish(g, carry):
        for slot in (1, 0):

            @pl.when(has_next(g, slot))
            def _():
                halo(g, slot).wait_send()

            @pl.when(has_before(g, slot))
            def _():
                term(g, slot).wait_send()

            @pl.when(returns(slot) & (g < HK - 1))
            def _():
                term_to_relay(g, slot).wait_send()

        @pl.when((half == 0) & (column == HK - 1) & (g > 0))
        def _():
            to_relay(g).wait_send()

        @pl.when(inner != g + FIRST_OWNER)
        def _():
            to_owner(g).wait_send()

        kept(g).wait()
        for p in near:
            placed(g, p).wait_send()
        for p in near:
            arrived(g, p).wait_recv()

        @pl.when(g == 0)
        def _():
            for part in range(2):
                for p in across:
                    early(part, p, me).wait_send()
                for p in across:
                    early(part, p, p).wait_recv()

        @pl.when(g > 0)
        def _():
            for p in across:
                placed(g, p).wait_send()
            for p in across:
                arrived(g, p).wait_recv()

        return carry

    with scope("finish"):
        lax.fori_loop(0, HK, finish, 0)
        result.wait()

    @pl.when(inner != HK + FIRST_OWNER)
    def _():
        to_owner(HK).wait_send()

    @pl.when(is_relay)
    def _():
        relayed(0).wait_send()

        @pl.when(core == 1)
        def _():
            relayed(1).wait_send()

    @pl.when(is_back_relay)
    def _():
        term_relayed(0).wait_send()

        @pl.when(core == 0)
        def _():
            term_relayed(1).wait_send()

    @pl.when(is_owner)
    def _():
        for j in range(1, 4):
            to_x(j).wait_send()
        for j in range(1, 8):
            to_z(j).wait_send()
            to_near(j).wait_send()


PARTS = 4


def lay_out(rows_ref, bias_ref, attn_ref, gq_ref, gk_ref, gv_ref, gb_ref, held, bias, in_s, out_s):
    wide = slice(0, HQ * HD)
    narrow = slice(HQ * HD, (HQ + HK) * HD)
    size = N // PARTS
    first = [pltpu.make_async_copy(bias_ref, bias, in_s.at[PARTS])]
    for i in range(PARTS):
        at = slice(i * size, (i + 1) * size)
        first.append(pltpu.make_async_copy(rows_ref.at[at], held.at[at], in_s.at[i]))
    for copy in first:
        copy.start()
    first[0].wait()
    then = [pltpu.make_async_copy(bias, gb_ref, out_s.at[PARTS, 0])]
    then[0].start()
    for i in range(PARTS):
        at = slice(i * size, (i + 1) * size)
        first[1 + i].wait()
        for n, (which, cols, ref) in enumerate(
            ((0, wide, attn_ref), (1, wide, gq_ref), (0, narrow, gk_ref), (1, narrow, gv_ref))
        ):
            copy = pltpu.make_async_copy(held.at[at, which, :, cols], ref.at[at], out_s.at[i, n])
            copy.start()
            then.append(copy)
    for copy in then:
        copy.wait()


def local(queries, keys, values, grad_out, doc_lengths, placement):
    vmem = pl.BlockSpec(memory_space=pltpu.VMEM)
    bf16, f32 = jnp.bfloat16, jnp.float32
    dma = pltpu.SemaphoreType.DMA
    rows, bias = pl.pallas_call(
        kernel,
        out_shape=(
            jax.ShapeDtypeStruct((N, 2, BLK, (HQ + HK) * HD), bf16),
            jax.ShapeDtypeStruct((SLICES, 8, HD), f32),
        ),
        in_specs=[pl.BlockSpec(memory_space=pltpu.HBM)] * 6,
        out_specs=(pl.BlockSpec(memory_space=pl.ANY), vmem),
        scratch_shapes=[
            pltpu.SMEM((1, N), jnp.int32),
            pltpu.SMEM((1, N, N), jnp.int32),
            pltpu.VMEM((ROWS, HQ * HD), bf16),
            pltpu.VMEM((ROWS, HK * HD), bf16),
            pltpu.VMEM((ROWS, HK * HD), bf16),
            pltpu.VMEM((ROWS, HQ * HD), bf16),
            dma((2 * HK + 4,)),
            pltpu.VMEM((N, 2, BLK, HK * HD), bf16),
            dma,
            pltpu.VMEM((HK, 3, 2, ROWS, HD), bf16),
            pltpu.VMEM((2, ROWS, HD), bf16),
            pltpu.VMEM((N, 2, BLK, HQ * HD), bf16),
            pltpu.VMEM((ROWS, ROWS), bf16),
            pltpu.VMEM((WIN, ROWS), f32),
            pltpu.VMEM((WIN, GROUP * ROWS), bf16),
            pltpu.VMEM((WIN, GROUP * ROWS), bf16),
            pltpu.VMEM((GROUP * ROWS, HD), bf16),
            pltpu.VMEM((HK, 2, 2, ROWS, HD), bf16),
            pltpu.VMEM((HK, 2, 2, ROWS, HD), bf16),
            pltpu.VMEM((2, 2, ROWS, HD), bf16),
            pltpu.VMEM((HK, 2, ROWS, HD), f32),
            pltpu.VMEM((HK, 2, 8, HD), f32),
            pltpu.VMEM((SLICES, 8, HD), f32),
            pltpu.VMEM((8, 8, HD), f32),
            pltpu.VMEM((4, 8, HD), f32),
            pltpu.VMEM((8, 8, HD), f32),
            pltpu.VMEM((SLICES, 8, HD), f32),
            dma((HK, 2)), dma((HK, 2)), dma((2,)), dma((1,)), dma((2,)), dma((2,)),
            dma((HK + 1, N)), dma((HK + 1, N)), dma((HK,)),
            dma((HK, 2)), dma((HK, 2)),
            dma((SLICES,)), dma((8,)), dma((4,)), dma((4,)),
            dma((8,)), dma((8,)), dma((8,)), dma((SLICES,)),
        ],
        compiler_params=pltpu.CompilerParams(
            collective_id=0, has_side_effects=True, vmem_limit_bytes=60 * 1024 * 1024
        ),
        cost_estimate=pl.CostEstimate(
            flops=2 * 6 * ROWS * HQ * HD * WIN,
            bytes_accessed=6 * 1024 * 1024,
            transcendentals=ROWS * HQ * WIN,
        ),
    )(doc_lengths, placement, queries[0], keys[0], values[0], grad_out[0])
    shape = jax.ShapeDtypeStruct
    results = pl.pallas_call(
        lay_out,
        out_shape=(
            shape((N, BLK, HQ * HD), bf16),
            shape((N, BLK, HQ * HD), bf16),
            shape((N, BLK, HK * HD), bf16),
            shape((N, BLK, HK * HD), bf16),
            shape((SLICES, 8, HD), f32),
        ),
        in_specs=[pl.BlockSpec(memory_space=pl.ANY)] * 2,
        out_specs=(pl.BlockSpec(memory_space=pl.ANY),) * 5,
        scratch_shapes=[
            pltpu.VMEM((N, 2, BLK, (HQ + HK) * HD), bf16),
            pltpu.VMEM((SLICES, 8, HD), f32),
            dma((PARTS + 1,)),
            dma((PARTS + 1, 4)),
        ],
        compiler_params=pltpu.CompilerParams(vmem_limit_bytes=60 * 1024 * 1024),
        cost_estimate=pl.CostEstimate(flops=0, bytes_accessed=5 * 1024 * 1024, transcendentals=0),
    )(rows, bias)
    return (
        results[0].reshape(1, ROWS, HQ * HD),
        results[1].reshape(1, ROWS, HQ * HD),
        results[2].reshape(1, ROWS, HK * HD),
        results[3].reshape(1, ROWS, HK * HD),
        results[4].reshape(SLICES * 8 * HD),
    )


def solution(mesh):
    return jax.shard_map(
        local,
        mesh=mesh,
        in_specs=(
            P("dp", "ctx", None),
            P("dp", "ctx", None),
            P("dp", "ctx", None),
            P("dp", "ctx", None),
            P("dp", None),
            P("dp", None, None),
        ),
        out_specs=(
            P("dp", "ctx", None),
            P("dp", "ctx", None),
            P("dp", "ctx", None),
            P("dp", "ctx", None),
            P(),
        ),
        check_vma=False,
    )
```

```python
import contextlib
import math

import jax
import jax.numpy as jnp
from jax import lax
from jax.experimental import pallas as pl
from jax.experimental.pallas import tpu as pltpu
from jax.sharding import PartitionSpec as P

HD = 128
HQ = 32
HK = 4
GROUP = HQ // HK
ROWS = 128
WIN = 384
BLK = 8
N = 16
MESH = pl.DeviceIdType.MESH
NT = (((1,), (1,)), ((), ()))
SCALE = 1.0 / math.sqrt(HD)
LOG2E = math.log2(math.e)
SLICES = HK + 1
FIRST_OWNER = 3
HELD = 3
KEEP = 4
EARLY = 2 * HD


SCOPES = False


def scope(name):
    return jax.named_scope(name) if SCOPES else contextlib.nullcontext()


def dot(a, b):
    return jnp.dot(a, b, preferred_element_type=jnp.float32)


def dot_nt(a, b):
    return lax.dot_general(a, b, NT, preferred_element_type=jnp.float32)


def halves(x):
    high = x.astype(jnp.bfloat16)
    return high, (x - high.astype(jnp.float32)).astype(jnp.bfloat16)


def kernel(
    len_hbm, place_hbm, q_hbm, k_hbm, v_hbm, do_hbm,
    rows_ref, bias_ref,
    len_ref, place_ref, q_ref, k_ref, v_ref, do_ref, in_s, gkv, gkv_s, win, win_relay, send, perm, mask,
    probs, dscore, ones, part, part_in, part_relay, own, colsum, bvec, b1, b2, b3, btot,
    halo_s, halo_r, pass_s, relay_s, relay_r, back_s, back_r, a2a_s, a2a_r, loc_s, part_s, part_r,
    p1_s, p1_r, p2_s, p2_r, p3_s, p3_r, p4_s, p4_r,
):
    me = lax.axis_index("ctx")
    seq = lax.axis_index("dp")
    half = me // 8
    inner = lax.rem(me, 8)

    x = seq // 4
    low = lax.rem(seq, 4)
    depth = half * 4 + low
    core = lax.rem(me, 2)

    across = [(1 - half) * 8 + lax.rem(inner + j, 8) for j in range(8)]
    near = [half * 8 + lax.rem(inner + j, 8) for j in range(1, 8)]
    peers = [{"ctx": p} for p in across + near]
    along_x = [{"dp": lax.rem(x + j, 4) * 4 + low} for j in range(1, 4)]
    along_z = []
    for j in range(1, 8):
        z = lax.rem(depth + j, 8)
        along_z.append({"ctx": (z // 4) * 8 + inner, "dp": x * 4 + lax.rem(z, 4)})
    others = peers + along_x + [along_z[j - 1] for j in range(1, 8) if j != 4]

    def remote(src, dst, send_sem, recv_sem, device):
        return pltpu.make_async_remote_copy(
            src_ref=src, dst_ref=dst, send_sem=send_sem, recv_sem=recv_sem,
            device_id=device, device_id_type=MESH,
        )

    def columns(g):
        return pl.ds(pl.multiple_of(g * GROUP * HD, GROUP * HD), GROUP * HD)

    def fetch_q(g):
        return pltpu.make_async_copy(q_hbm.at[:, columns(g)], q_ref.at[:, columns(g)], in_s.at[g])

    def fetch_do(g):
        return pltpu.make_async_copy(
            do_hbm.at[:, columns(g)], do_ref.at[:, columns(g)], in_s.at[HK + g]
        )

    small = [
        pltpu.make_async_copy(src, dst, in_s.at[2 * HK + i])
        for i, (src, dst) in enumerate(
            ((k_hbm, k_ref), (v_hbm, v_ref), (len_hbm, len_ref), (place_hbm, place_ref))
        )
    ]
    with scope("signals"):
        for copy in small:
            copy.start()
        barrier = pltpu.get_barrier_semaphore()
        for device in others:
            pl.semaphore_signal(barrier, inc=1, device_id=device, device_id_type=MESH)
        for g in range(HK):
            fetch_q(g).start()
            fetch_do(g).start()
        for copy in small:
            copy.wait()

    for g in range(HK):
        win[g, 2, 0] = k_ref[:, g * HD : (g + 1) * HD]
        win[g, 2, 1] = v_ref[:, g * HD : (g + 1) * HD]

    @pl.when(me < 2)
    def _():
        win[:, 0] = jnp.zeros((HK, 2, ROWS, HD), jnp.bfloat16)

    @pl.when(me < 1)
    def _():
        win[:, 1] = jnp.zeros((HK, 2, ROWS, HD), jnp.bfloat16)

    with scope("barrier"):
        pl.semaphore_wait(barrier, len(others))

    def halo(g, slot):
        return remote(
            win.at[g, 2], win.at[g, slot], halo_s.at[g, slot], halo_r.at[g, slot],
            {"ctx": lax.rem(me + (2 - slot), N)},
        )

    def term(g, slot):
        return remote(
            part.at[g, slot], part_in.at[g, slot], part_s.at[g, slot], part_r.at[g, slot],
            {"ctx": lax.rem(me + N - (2 - slot), N)},
        )

    column = inner // 2
    relay_head = HK - 1 - column

    def leaves(slot):
        return (half == 0) & (me + (2 - slot) >= 8)

    def returns(slot):
        return (half == 1) & (me - (2 - slot) < 8)

    def has_next(g, slot):
        direct = jnp.logical_not(leaves(slot)) | ((g == 0) & (inner == 6 + slot))
        return (me + (2 - slot) < N) & direct

    def to_relay(g):
        return remote(
            win.at[g, 2], win_relay, halo_s.at[g, 0], relay_r.at[0],
            {"ctx": 2 * (HK - 1 - g) + core},
        )

    def relayed():
        return remote(
            win_relay, win.at[relay_head, core], relay_s.at[0], halo_r.at[relay_head, core],
            {"ctx": 8},
        )

    def handed(g):
        return remote(
            win.at[g, 1], win.at[g, 0], pass_s.at[g], halo_r.at[g, 0], {"ctx": 9}
        )

    is_relay = (half == 0) & (column < HK - 1)

    with scope("halo_start"):
        for g in range(HK):
            for slot in (1, 0):

                @pl.when(has_next(g, slot))
                def _():
                    halo(g, slot).start()

            if g > 0:

                @pl.when((half == 0) & (column == HK - 1))
                def _():
                    to_relay(g).start()

        @pl.when(is_relay)
        def _():
            to_relay(1).wait_recv()
            relayed().start()

    lane = lax.broadcasted_iota(jnp.int32, (1, ROWS), 1)
    pos = me * ROWS + lane
    first = jnp.zeros((1, ROWS), jnp.int32)
    start = len_ref[0, 0] * 0
    for i in range(N):
        first = jnp.where(pos >= start, start, first)
        start = start + len_ref[0, i]
    t_pos = (me - 2) * ROWS + lax.broadcasted_iota(jnp.int32, (WIN, ROWS), 0)
    seen = (t_pos >= first) & (t_pos <= pos)
    mask[...] = jnp.where(seen, 0.0, -1e30)

    target = lax.rem(lane, BLK)
    for j in range(N):
        target = target + jnp.where(lane // BLK == j, place_ref[0, me, j] * BLK, 0)
    row = lax.broadcasted_iota(jnp.int32, (ROWS, ROWS), 0)
    perm[...] = jnp.where(row == target, 1.0, 0.0).astype(jnp.bfloat16)
    ones[...] = jnp.where(
        lax.broadcasted_iota(jnp.int32, (GROUP * ROWS, HD), 0) // ROWS
        == lax.broadcasted_iota(jnp.int32, (GROUP * ROWS, HD), 1),
        1.0, 0.0,
    ).astype(jnp.bfloat16)

    def has_before(g, slot):
        return (me >= 2 - slot) & (jnp.logical_not(returns(slot)) | (g == HK - 1))

    def term_to_relay(g, slot):
        return remote(
            part.at[g, slot], part_relay.at[slot], part_s.at[g, slot], back_r.at[slot],
            {"ctx": 8 + 2 * (HK - 1 - g) + core},
        )

    def term_relayed(slot):
        return remote(
            part_relay.at[slot], part_in.at[relay_head, slot], back_s.at[slot],
            part_r.at[relay_head, slot], {"ctx": 8 + core - (2 - slot)},
        )

    is_back_relay = (half == 1) & (column > 0)

    def placed(g, p):
        cols = columns(g)
        return remote(
            send.at[p, :, :, cols], rows_ref.at[me, :, :, cols], a2a_s.at[g, p], a2a_r.at[g, me],
            {"ctx": p},
        )

    def arrived(g, p):
        cols = columns(g)
        return remote(
            send.at[p, :, :, cols], rows_ref.at[p, :, :, cols], a2a_s.at[g, p], a2a_r.at[g, p],
            {"ctx": p},
        )

    def early(part, p, source):
        cols = (slice(0, EARLY), slice(EARLY, GROUP * HD))[part]
        i = (HK, 0)[part]
        return remote(
            send.at[p, :, :, cols], rows_ref.at[source, :, :, cols], a2a_s.at[i, p],
            a2a_r.at[i, source], {"ctx": p},
        )

    def kept(g):
        cols = columns(g)
        return pltpu.make_async_copy(
            send.at[me, :, :, cols], rows_ref.at[me, :, :, cols], loc_s.at[g]
        )

    def to_owner(s):
        return remote(
            bvec.at[s], b1.at[inner], p1_s.at[s], p1_r.at[inner],
            {"ctx": half * 8 + s + FIRST_OWNER},
        )

    is_owner = inner >= FIRST_OWNER
    is_held = inner >= 2

    def group_step(g, carry):
        with scope("halo"):
            fetch_q(g).wait()
            fetch_do(g).wait()
            for slot in (1, 0):

                @pl.when(me >= 2 - slot)
                def _():
                    halo(g, slot).wait_recv()

                if slot == 1:

                    @pl.when(me == 8)
                    def _():
                        handed(g).start()

        keys = win[g, :, 0].reshape(WIN, HD)
        values = win[g, :, 1].reshape(WIN, HD)
        keys_t = keys.astype(jnp.float32).T.astype(jnp.bfloat16)
        values_t = values.astype(jnp.float32).T.astype(jnp.bfloat16)
        shut = jnp.concatenate([mask[...], mask[...]], axis=1)

        def stacked(ref, first_head, count):
            cols = pl.ds(pl.multiple_of((g * GROUP + first_head) * HD, HD), count * HD)
            x = ref[:, cols]
            return jnp.concatenate([x[:, i * HD : (i + 1) * HD] for i in range(count)], axis=0)

        with scope("heads"):
            def products(pair):
                q2 = stacked(q_ref, pair * 2, 2)
                do2 = stacked(do_ref, pair * 2, 2)
                return dot_nt(keys, q2) + shut, dot_nt(values, do2)

            ahead = products(0)
            for pair in range(GROUP // 2):
                scores, grad = ahead
                if pair + 1 < GROUP // 2:
                    ahead = products(pair + 1)
                top = jnp.max(scores, axis=0, keepdims=True)
                e = jnp.exp2((scores - top) * (SCALE * LOG2E))
                inv = 1.0 / jnp.sum(e, axis=0, keepdims=True)
                weights = (e * inv).astype(jnp.bfloat16)
                delta = jnp.sum(weights.astype(jnp.float32) * grad, axis=0, keepdims=True)
                ds = (e * (inv * SCALE) * (grad - delta)).astype(jnp.bfloat16)
                at = slice(pair * 2 * ROWS, (pair + 1) * 2 * ROWS)
                probs[:, at] = weights
                dscore[:, at] = ds
                cols = pl.ds(pl.multiple_of((g * GROUP + pair * 2) * HD, 2 * HD), 2 * HD)
                for i, out_t in enumerate((dot(values_t, weights), dot(keys_t, ds))):
                    out_t = out_t.astype(jnp.bfloat16)
                    out = dot_nt(
                        perm[...], jnp.concatenate([out_t[:, :ROWS], out_t[:, ROWS:]], axis=0)
                    )
                    send[:, i, :, cols] = out.reshape(N, BLK, 2 * HD).astype(jnp.bfloat16)

                if (pair + 1) * 2 * HD == EARLY:

                    @pl.when(g == 0)
                    def _():
                        for p in across:
                            early(0, p, me).start()

        with scope("sends"):

            @pl.when(g == 0)
            def _():
                for p in across:
                    early(1, p, me).start()

            @pl.when((g > 0) & ((g < HELD) | jnp.logical_not(is_held | (half == 1))))
            def _():
                for p in across:
                    placed(g, p).start()


        with scope("terms"):
            dv = dot(probs[...], stacked(do_ref, 0, GROUP))
            both = jnp.concatenate([stacked(q_ref, 0, GROUP), ones[...]], axis=1)
            dk = dot(dscore[...], both)
            part[g, :, 0] = dk[: 2 * ROWS, :HD].reshape(2, ROWS, HD).astype(jnp.bfloat16)
            part[g, :, 1] = dv[: 2 * ROWS].reshape(2, ROWS, HD).astype(jnp.bfloat16)
            for slot in (1, 0):

                @pl.when(has_before(g, slot))
                def _():
                    term(g, slot).start()

                @pl.when(returns(slot) & (g < HK - 1))
                def _():
                    term_to_relay(g, slot).start()

            own[g, 0] = dk[2 * ROWS :, :HD]
            own[g, 1] = dv[2 * ROWS :]
            colsum[g, 0] = jnp.broadcast_to(jnp.sum(dk[:, :HD], axis=0, keepdims=True), (8, HD))
            colsum[g, 1] = jnp.broadcast_to(jnp.sum(dv, axis=0, keepdims=True), (8, HD))
            high, low = halves(dk[:, HD:])
            query_sum = dot(keys_t, high) + dot(keys_t, low)
            bvec[g] = query_sum.T[:GROUP]

            @pl.when(inner != g + FIRST_OWNER)
            def _():
                to_owner(g).start()

        @pl.when((g >= HELD) & jnp.logical_not(is_held) & (half == 1))
        def _():
            for p in across[:KEEP]:
                placed(g, p).start()

        @pl.when((g >= HELD) & (is_held | (half == 1)))
        def _():
            for p in across[KEEP:]:
                placed(g, p).start()

        for p in near:
            placed(g, p).start()
        kept(g).start()
        return carry

    lax.fori_loop(0, HK, group_step, 0)

    for g in range(HK):
        bvec[HK, g : g + 1] = colsum[g, 0, :1]
        bvec[HK, HK + g : HK + g + 1] = colsum[g, 1, :1]

    @pl.when(inner != HK + FIRST_OWNER)
    def _():
        to_owner(HK).start()

    mine = inner - FIRST_OWNER

    def to_x(j):
        return remote(b2.at[x], b2.at[x], p2_s.at[j], p2_r.at[x], along_x[j - 1])

    def from_x(j):
        at = lax.rem(x + j, 4)
        return remote(b2.at[at], b2.at[at], p2_s.at[j], p2_r.at[at], along_x[j - 1])

    def to_z(j):
        return remote(b3.at[depth], b3.at[depth], p3_s.at[j], p3_r.at[depth], along_z[j - 1])

    def from_z(j):
        at = lax.rem(depth + j, 8)
        return remote(b3.at[at], b3.at[at], p3_s.at[j], p3_r.at[at], along_z[j - 1])

    def to_near(j):
        device = {"ctx": near[j - 1]}
        return remote(btot.at[mine], btot.at[mine], p4_s.at[j], p4_r.at[mine], device)

    with scope("owner"):

        @pl.when(is_owner)
        def _():
            b1[inner] = bvec[mine]
            for j in range(1, 8):
                at = lax.rem(inner + j, 8)
                remote(
                    bvec.at[mine], b1.at[at], p1_s.at[mine], p1_r.at[at], {"ctx": near[j - 1]}
                ).wait_recv()
            total = b1[0]
            for j in range(1, 8):
                total = total + b1[j]
            b2[x] = total
            for j in range(1, 4):
                to_x(j).start()
            for j in range(1, 4):
                from_x(j).wait_recv()
            b3[depth] = (b2[0] + b2[1]) + (b2[2] + b2[3])
            for j in range(1, 8):
                to_z(j).start()

    with scope("relay"):

        @pl.when(is_back_relay)
        def _():
            term_to_relay(0, 0).wait_recv()
            term_relayed(0).start()

            @pl.when(core == 0)
            def _():
                term_to_relay(0, 1).wait_recv()
                term_relayed(1).start()

    @pl.when(is_held)
    def _():
        for g in range(HELD, HK):
            for p in across[:KEEP]:
                placed(g, p).start()

    with scope("total"):

        @pl.when(is_owner)
        def _():
            for j in range(1, 8):
                from_z(j).wait_recv()
            total = b3[0]
            for j in range(1, 8):
                total = total + b3[j]
            btot[mine] = total
            for j in range(1, 8):
                to_near(j).start()

    with scope("bias"):
        for s in range(SLICES):

            @pl.when(inner != s + FIRST_OWNER)
            def _():
                remote(
                    btot.at[s], btot.at[s], p4_s.at[0], p4_r.at[s],
                    {"ctx": half * 8 + s + FIRST_OWNER},
                ).wait_recv()

    bias_ref[...] = btot[...]

    with scope("gkv"):
        for g in range(HK):
            for slot in (1, 0):

                @pl.when(me + (2 - slot) < N)
                def _():
                    term(g, slot).wait_recv()

                @pl.when(me + (2 - slot) >= N)
                def _():
                    part_in[g, slot] = jnp.zeros((2, ROWS, HD), jnp.bfloat16)

            for i in range(2):
                total = own[g, i] + part_in[g, 1, i].astype(jnp.float32)
                total = total + part_in[g, 0, i].astype(jnp.float32)
                gkv[:, i, :, g * HD : (g + 1) * HD] = total.reshape(N, BLK, HD).astype(
                    jnp.bfloat16
                )
        result = pltpu.make_async_copy(gkv, rows_ref.at[:, :, :, HQ * HD :], gkv_s)
        result.start()

    def finish(g, carry):
        for slot in (1, 0):

            @pl.when(has_next(g, slot))
            def _():
                halo(g, slot).wait_send()

            @pl.when(has_before(g, slot))
            def _():
                term(g, slot).wait_send()

            @pl.when(returns(slot) & (g < HK - 1))
            def _():
                term_to_relay(g, slot).wait_send()

        @pl.when((half == 0) & (column == HK - 1) & (g > 0))
        def _():
            to_relay(g).wait_send()

        @pl.when(me == 8)
        def _():
            handed(g).wait_send()

        @pl.when(inner != g + FIRST_OWNER)
        def _():
            to_owner(g).wait_send()

        kept(g).wait()
        for p in near:
            placed(g, p).wait_send()
        for p in near:
            arrived(g, p).wait_recv()

        @pl.when(g == 0)
        def _():
            for part in range(2):
                for p in across:
                    early(part, p, me).wait_send()
                for p in across:
                    early(part, p, p).wait_recv()

        @pl.when(g > 0)
        def _():
            for p in across:
                placed(g, p).wait_send()
            for p in across:
                arrived(g, p).wait_recv()

        return carry

    with scope("finish"):
        lax.fori_loop(0, HK, finish, 0)
        result.wait()

    @pl.when(inner != HK + FIRST_OWNER)
    def _():
        to_owner(HK).wait_send()

    @pl.when(is_relay)
    def _():
        relayed().wait_send()

    @pl.when(is_back_relay)
    def _():
        term_relayed(0).wait_send()

        @pl.when(core == 0)
        def _():
            term_relayed(1).wait_send()

    @pl.when(is_owner)
    def _():
        for j in range(1, 4):
            to_x(j).wait_send()
        for j in range(1, 8):
            to_z(j).wait_send()
            to_near(j).wait_send()


PARTS = 4


def lay_out(rows_ref, bias_ref, attn_ref, gq_ref, gk_ref, gv_ref, gb_ref, held, bias, in_s, out_s):
    wide = slice(0, HQ * HD)
    narrow = slice(HQ * HD, (HQ + HK) * HD)
    size = N // PARTS
    first = [pltpu.make_async_copy(bias_ref, bias, in_s.at[PARTS])]
    for i in range(PARTS):
        at = slice(i * size, (i + 1) * size)
        first.append(pltpu.make_async_copy(rows_ref.at[at], held.at[at], in_s.at[i]))
    for copy in first:
        copy.start()
    first[0].wait()
    then = [pltpu.make_async_copy(bias, gb_ref, out_s.at[PARTS, 0])]
    then[0].start()
    for i in range(PARTS):
        at = slice(i * size, (i + 1) * size)
        first[1 + i].wait()
        for n, (which, cols, ref) in enumerate(
            ((0, wide, attn_ref), (1, wide, gq_ref), (0, narrow, gk_ref), (1, narrow, gv_ref))
        ):
            copy = pltpu.make_async_copy(held.at[at, which, :, cols], ref.at[at], out_s.at[i, n])
            copy.start()
            then.append(copy)
    for copy in then:
        copy.wait()


def local(queries, keys, values, grad_out, doc_lengths, placement):
    vmem = pl.BlockSpec(memory_space=pltpu.VMEM)
    bf16, f32 = jnp.bfloat16, jnp.float32
    dma = pltpu.SemaphoreType.DMA
    rows, bias = pl.pallas_call(
        kernel,
        out_shape=(
            jax.ShapeDtypeStruct((N, 2, BLK, (HQ + HK) * HD), bf16),
            jax.ShapeDtypeStruct((SLICES, 8, HD), f32),
        ),
        in_specs=[pl.BlockSpec(memory_space=pltpu.HBM)] * 6,
        out_specs=(pl.BlockSpec(memory_space=pl.ANY), vmem),
        scratch_shapes=[
            pltpu.SMEM((1, N), jnp.int32),
            pltpu.SMEM((1, N, N), jnp.int32),
            pltpu.VMEM((ROWS, HQ * HD), bf16),
            pltpu.VMEM((ROWS, HK * HD), bf16),
            pltpu.VMEM((ROWS, HK * HD), bf16),
            pltpu.VMEM((ROWS, HQ * HD), bf16),
            dma((2 * HK + 4,)),
            pltpu.VMEM((N, 2, BLK, HK * HD), bf16),
            dma,
            pltpu.VMEM((HK, 3, 2, ROWS, HD), bf16),
            pltpu.VMEM((2, ROWS, HD), bf16),
            pltpu.VMEM((N, 2, BLK, HQ * HD), bf16),
            pltpu.VMEM((ROWS, ROWS), bf16),
            pltpu.VMEM((WIN, ROWS), f32),
            pltpu.VMEM((WIN, GROUP * ROWS), bf16),
            pltpu.VMEM((WIN, GROUP * ROWS), bf16),
            pltpu.VMEM((GROUP * ROWS, HD), bf16),
            pltpu.VMEM((HK, 2, 2, ROWS, HD), bf16),
            pltpu.VMEM((HK, 2, 2, ROWS, HD), bf16),
            pltpu.VMEM((2, 2, ROWS, HD), bf16),
            pltpu.VMEM((HK, 2, ROWS, HD), f32),
            pltpu.VMEM((HK, 2, 8, HD), f32),
            pltpu.VMEM((SLICES, 8, HD), f32),
            pltpu.VMEM((8, 8, HD), f32),
            pltpu.VMEM((4, 8, HD), f32),
            pltpu.VMEM((8, 8, HD), f32),
            pltpu.VMEM((SLICES, 8, HD), f32),
            dma((HK, 2)), dma((HK, 2)), dma((HK,)), dma((1,)), dma((1,)), dma((2,)), dma((2,)),
            dma((HK + 1, N)), dma((HK + 1, N)), dma((HK,)),
            dma((HK, 2)), dma((HK, 2)),
            dma((SLICES,)), dma((8,)), dma((4,)), dma((4,)),
            dma((8,)), dma((8,)), dma((8,)), dma((SLICES,)),
        ],
        compiler_params=pltpu.CompilerParams(
            collective_id=0, has_side_effects=True, vmem_limit_bytes=60 * 1024 * 1024
        ),
        cost_estimate=pl.CostEstimate(
            flops=2 * 6 * ROWS * HQ * HD * WIN,
            bytes_accessed=6 * 1024 * 1024,
            transcendentals=ROWS * HQ * WIN,
        ),
    )(doc_lengths, placement, queries[0], keys[0], values[0], grad_out[0])
    shape = jax.ShapeDtypeStruct
    results = pl.pallas_call(
        lay_out,
        out_shape=(
            shape((N, BLK, HQ * HD), bf16),
            shape((N, BLK, HQ * HD), bf16),
            shape((N, BLK, HK * HD), bf16),
            shape((N, BLK, HK * HD), bf16),
            shape((SLICES, 8, HD), f32),
        ),
        in_specs=[pl.BlockSpec(memory_space=pl.ANY)] * 2,
        out_specs=(pl.BlockSpec(memory_space=pl.ANY),) * 5,
        scratch_shapes=[
            pltpu.VMEM((N, 2, BLK, (HQ + HK) * HD), bf16),
            pltpu.VMEM((SLICES, 8, HD), f32),
            dma((PARTS + 1,)),
            dma((PARTS + 1, 4)),
        ],
        compiler_params=pltpu.CompilerParams(vmem_limit_bytes=60 * 1024 * 1024),
        cost_estimate=pl.CostEstimate(flops=0, bytes_accessed=5 * 1024 * 1024, transcendentals=0),
    )(rows, bias)
    return (
        results[0].reshape(1, ROWS, HQ * HD),
        results[1].reshape(1, ROWS, HQ * HD),
        results[2].reshape(1, ROWS, HK * HD),
        results[3].reshape(1, ROWS, HK * HD),
        results[4].reshape(SLICES * 8 * HD),
    )


def solution(mesh):
    return jax.shard_map(
        local,
        mesh=mesh,
        in_specs=(
            P("dp", "ctx", None),
            P("dp", "ctx", None),
            P("dp", "ctx", None),
            P("dp", "ctx", None),
            P("dp", None),
            P("dp", None, None),
        ),
        out_specs=(
            P("dp", "ctx", None),
            P("dp", "ctx", None),
            P("dp", "ctx", None),
            P("dp", "ctx", None),
            P(),
        ),
        check_vma=False,
    )
```

```python
import contextlib
import math

import jax
import jax.numpy as jnp
from jax import lax
from jax.experimental import pallas as pl
from jax.experimental.pallas import tpu as pltpu
from jax.sharding import PartitionSpec as P

HD = 128
HQ = 32
HK = 4
GROUP = HQ // HK
ROWS = 128
WIN = 384
BLK = 8
N = 16
MESH = pl.DeviceIdType.MESH
NT = (((1,), (1,)), ((), ()))
SCALE = 1.0 / math.sqrt(HD)
LOG2E = math.log2(math.e)
SLICES = HK + 1
FIRST_OWNER = 2
HELD = 3
KEEP = 4
EARLY = 2 * HD


SCOPES = False


def scope(name):
    return jax.named_scope(name) if SCOPES else contextlib.nullcontext()


def dot(a, b):
    return jnp.dot(a, b, preferred_element_type=jnp.float32)


def dot_nt(a, b):
    return lax.dot_general(a, b, NT, preferred_element_type=jnp.float32)


def halves(x):
    high = x.astype(jnp.bfloat16)
    return high, (x - high.astype(jnp.float32)).astype(jnp.bfloat16)


def kernel(
    len_hbm, place_hbm, q_hbm, k_hbm, v_hbm, do_hbm,
    rows_ref, bias_ref,
    len_ref, place_ref, q_ref, k_ref, v_ref, do_ref, in_s, gkv, gkv_s, win, win_relay, send, perm, mask,
    probs, dscore, ones, part, part_in, part_relay, own, colsum, bvec, b1, b2, b3, btot,
    halo_s, halo_r, pass_s, relay_s, relay_r, back_s, back_r, a2a_s, a2a_r, loc_s, part_s, part_r,
    p1_s, p1_r, p2_s, p2_r, p3_s, p3_r, p4_s, p4_r,
):
    me = lax.axis_index("ctx")
    seq = lax.axis_index("dp")
    half = me // 8
    inner = lax.rem(me, 8)

    x = seq // 4
    low = lax.rem(seq, 4)
    depth = half * 4 + low
    core = lax.rem(me, 2)

    across = [(1 - half) * 8 + lax.rem(inner + j, 8) for j in range(8)]
    near = [half * 8 + lax.rem(inner + j, 8) for j in range(1, 8)]
    peers = [{"ctx": p} for p in across + near]
    along_x = [{"dp": lax.rem(x + j, 4) * 4 + low} for j in range(1, 4)]
    along_z = []
    for j in range(1, 8):
        z = lax.rem(depth + j, 8)
        along_z.append({"ctx": (z // 4) * 8 + inner, "dp": x * 4 + lax.rem(z, 4)})
    others = peers + along_x + [along_z[j - 1] for j in range(1, 8) if j != 4]

    def remote(src, dst, send_sem, recv_sem, device):
        return pltpu.make_async_remote_copy(
            src_ref=src, dst_ref=dst, send_sem=send_sem, recv_sem=recv_sem,
            device_id=device, device_id_type=MESH,
        )

    def columns(g):
        return pl.ds(pl.multiple_of(g * GROUP * HD, GROUP * HD), GROUP * HD)

    def fetch_q(g):
        return pltpu.make_async_copy(q_hbm.at[:, columns(g)], q_ref.at[:, columns(g)], in_s.at[g])

    def fetch_do(g):
        return pltpu.make_async_copy(
            do_hbm.at[:, columns(g)], do_ref.at[:, columns(g)], in_s.at[HK + g]
        )

    small = [
        pltpu.make_async_copy(src, dst, in_s.at[2 * HK + i])
        for i, (src, dst) in enumerate(
            ((k_hbm, k_ref), (v_hbm, v_ref), (len_hbm, len_ref), (place_hbm, place_ref))
        )
    ]
    with scope("signals"):
        for copy in small:
            copy.start()
        barrier = pltpu.get_barrier_semaphore()
        for device in others:
            pl.semaphore_signal(barrier, inc=1, device_id=device, device_id_type=MESH)
        for g in range(HK):
            fetch_q(g).start()
            fetch_do(g).start()
        for copy in small:
            copy.wait()

    for g in range(HK):
        win[g, 2, 0] = k_ref[:, g * HD : (g + 1) * HD]
        win[g, 2, 1] = v_ref[:, g * HD : (g + 1) * HD]

    @pl.when(me < 2)
    def _():
        win[:, 0] = jnp.zeros((HK, 2, ROWS, HD), jnp.bfloat16)

    @pl.when(me < 1)
    def _():
        win[:, 1] = jnp.zeros((HK, 2, ROWS, HD), jnp.bfloat16)

    with scope("barrier"):
        pl.semaphore_wait(barrier, len(others))

    def halo(g, slot):
        return remote(
            win.at[g, 2], win.at[g, slot], halo_s.at[g, slot], halo_r.at[g, slot],
            {"ctx": lax.rem(me + (2 - slot), N)},
        )

    def term(g, slot):
        return remote(
            part.at[g, slot], part_in.at[g, slot], part_s.at[g, slot], part_r.at[g, slot],
            {"ctx": lax.rem(me + N - (2 - slot), N)},
        )

    column = inner // 2
    relay_head = HK - 1 - column

    def leaves(slot):
        return (half == 0) & (me + (2 - slot) >= 8)

    def returns(slot):
        return (half == 1) & (me - (2 - slot) < 8)

    def has_next(g, slot):
        direct = jnp.logical_not(leaves(slot)) | ((g == 0) & (inner == 6 + slot))
        return (me + (2 - slot) < N) & direct

    def to_relay(g):
        return remote(
            win.at[g, 2], win_relay, halo_s.at[g, 0], relay_r.at[0],
            {"ctx": 2 * (HK - 1 - g) + core},
        )

    def relayed():
        return remote(
            win_relay, win.at[relay_head, core], relay_s.at[0], halo_r.at[relay_head, core],
            {"ctx": 8},
        )

    def handed(g):
        return remote(
            win.at[g, 1], win.at[g, 0], pass_s.at[g], halo_r.at[g, 0], {"ctx": 9}
        )

    is_relay = (half == 0) & (column < HK - 1)

    with scope("halo_start"):
        for g in range(HK):
            for slot in (1, 0):

                @pl.when(has_next(g, slot))
                def _():
                    halo(g, slot).start()

            if g > 0:

                @pl.when((half == 0) & (column == HK - 1))
                def _():
                    to_relay(g).start()

        @pl.when(is_relay)
        def _():
            to_relay(1).wait_recv()
            relayed().start()

    lane = lax.broadcasted_iota(jnp.int32, (1, ROWS), 1)
    pos = me * ROWS + lane
    first = jnp.zeros((1, ROWS), jnp.int32)
    start = len_ref[0, 0] * 0
    for i in range(N):
        first = jnp.where(pos >= start, start, first)
        start = start + len_ref[0, i]
    t_pos = (me - 2) * ROWS + lax.broadcasted_iota(jnp.int32, (WIN, ROWS), 0)
    seen = (t_pos >= first) & (t_pos <= pos)
    mask[...] = jnp.where(seen, 0.0, -1e30)

    target = lax.rem(lane, BLK)
    for j in range(N):
        target = target + jnp.where(lane // BLK == j, place_ref[0, me, j] * BLK, 0)
    row = lax.broadcasted_iota(jnp.int32, (ROWS, ROWS), 0)
    perm[...] = jnp.where(row == target, 1.0, 0.0).astype(jnp.bfloat16)
    ones[...] = jnp.where(
        lax.broadcasted_iota(jnp.int32, (GROUP * ROWS, HD), 0) // ROWS
        == lax.broadcasted_iota(jnp.int32, (GROUP * ROWS, HD), 1),
        1.0, 0.0,
    ).astype(jnp.bfloat16)

    def has_before(g, slot):
        return (me >= 2 - slot) & (jnp.logical_not(returns(slot)) | (g == HK - 1))

    def term_to_relay(g, slot):
        return remote(
            part.at[g, slot], part_relay.at[slot], part_s.at[g, slot], back_r.at[slot],
            {"ctx": 8 + 2 * (HK - 1 - g) + core},
        )

    def term_relayed(slot):
        return remote(
            part_relay.at[slot], part_in.at[relay_head, slot], back_s.at[slot],
            part_r.at[relay_head, slot], {"ctx": 8 + core - (2 - slot)},
        )

    is_back_relay = (half == 1) & (column > 0)

    def placed(g, p):
        cols = columns(g)
        return remote(
            send.at[p, :, :, cols], rows_ref.at[me, :, :, cols], a2a_s.at[g, p], a2a_r.at[g, me],
            {"ctx": p},
        )

    def arrived(g, p):
        cols = columns(g)
        return remote(
            send.at[p, :, :, cols], rows_ref.at[p, :, :, cols], a2a_s.at[g, p], a2a_r.at[g, p],
            {"ctx": p},
        )

    def early(part, p, source):
        cols = (slice(0, EARLY), slice(EARLY, GROUP * HD))[part]
        i = (HK, 0)[part]
        return remote(
            send.at[p, :, :, cols], rows_ref.at[source, :, :, cols], a2a_s.at[i, p],
            a2a_r.at[i, source], {"ctx": p},
        )

    def kept(g):
        cols = columns(g)
        return pltpu.make_async_copy(
            send.at[me, :, :, cols], rows_ref.at[me, :, :, cols], loc_s.at[g]
        )

    def to_owner(s):
        return remote(
            bvec.at[s], b1.at[inner], p1_s.at[s], p1_r.at[inner],
            {"ctx": half * 8 + s + FIRST_OWNER},
        )

    is_owner = (inner >= FIRST_OWNER) & (inner < FIRST_OWNER + SLICES)
    is_held = inner >= 2

    def group_step(g, carry):
        with scope("halo"):
            fetch_q(g).wait()
            fetch_do(g).wait()
            for slot in (1, 0):

                @pl.when(me >= 2 - slot)
                def _():
                    halo(g, slot).wait_recv()

                if slot == 1:

                    @pl.when(me == 8)
                    def _():
                        handed(g).start()

        keys = win[g, :, 0].reshape(WIN, HD)
        values = win[g, :, 1].reshape(WIN, HD)
        keys_t = keys.astype(jnp.float32).T.astype(jnp.bfloat16)
        values_t = values.astype(jnp.float32).T.astype(jnp.bfloat16)
        shut = jnp.concatenate([mask[...], mask[...]], axis=1)

        def stacked(ref, first_head, count):
            cols = pl.ds(pl.multiple_of((g * GROUP + first_head) * HD, HD), count * HD)
            x = ref[:, cols]
            return jnp.concatenate([x[:, i * HD : (i + 1) * HD] for i in range(count)], axis=0)

        with scope("heads"):
            def products(pair):
                q2 = stacked(q_ref, pair * 2, 2)
                do2 = stacked(do_ref, pair * 2, 2)
                return dot_nt(keys, q2) + shut, dot_nt(values, do2)

            ahead = products(0)
            for pair in range(GROUP // 2):
                scores, grad = ahead
                if pair + 1 < GROUP // 2:
                    ahead = products(pair + 1)
                top = jnp.max(scores, axis=0, keepdims=True)
                e = jnp.exp2((scores - top) * (SCALE * LOG2E))
                inv = 1.0 / jnp.sum(e, axis=0, keepdims=True)
                weights = (e * inv).astype(jnp.bfloat16)
                delta = jnp.sum(weights.astype(jnp.float32) * grad, axis=0, keepdims=True)
                ds = (e * (inv * SCALE) * (grad - delta)).astype(jnp.bfloat16)
                at = slice(pair * 2 * ROWS, (pair + 1) * 2 * ROWS)
                probs[:, at] = weights
                dscore[:, at] = ds
                cols = pl.ds(pl.multiple_of((g * GROUP + pair * 2) * HD, 2 * HD), 2 * HD)
                for i, out_t in enumerate((dot(values_t, weights), dot(keys_t, ds))):
                    out_t = out_t.astype(jnp.bfloat16)
                    out = dot_nt(
                        perm[...], jnp.concatenate([out_t[:, :ROWS], out_t[:, ROWS:]], axis=0)
                    )
                    send[:, i, :, cols] = out.reshape(N, BLK, 2 * HD).astype(jnp.bfloat16)

                if (pair + 1) * 2 * HD == EARLY:

                    @pl.when(g == 0)
                    def _():
                        for p in across:
                            early(0, p, me).start()

        with scope("sends"):

            @pl.when(g == 0)
            def _():
                for p in across:
                    early(1, p, me).start()

            @pl.when((g > 0) & ((g < HELD) | jnp.logical_not(is_held | (half == 1))))
            def _():
                for p in across:
                    placed(g, p).start()


        with scope("terms"):
            dv = dot(probs[...], stacked(do_ref, 0, GROUP))
            both = jnp.concatenate([stacked(q_ref, 0, GROUP), ones[...]], axis=1)
            dk = dot(dscore[...], both)
            part[g, :, 0] = dk[: 2 * ROWS, :HD].reshape(2, ROWS, HD).astype(jnp.bfloat16)
            part[g, :, 1] = dv[: 2 * ROWS].reshape(2, ROWS, HD).astype(jnp.bfloat16)
            for slot in (1, 0):

                @pl.when(has_before(g, slot))
                def _():
                    term(g, slot).start()

                @pl.when(returns(slot) & (g < HK - 1))
                def _():
                    term_to_relay(g, slot).start()

            own[g, 0] = dk[2 * ROWS :, :HD]
            own[g, 1] = dv[2 * ROWS :]
            colsum[g, 0] = jnp.broadcast_to(jnp.sum(dk[:, :HD], axis=0, keepdims=True), (8, HD))
            colsum[g, 1] = jnp.broadcast_to(jnp.sum(dv, axis=0, keepdims=True), (8, HD))
            high, low = halves(dk[:, HD:])
            query_sum = dot(keys_t, high) + dot(keys_t, low)
            bvec[g] = query_sum.T[:GROUP]

            @pl.when(inner != g + FIRST_OWNER)
            def _():
                to_owner(g).start()

        @pl.when((g >= HELD) & jnp.logical_not(is_held) & (half == 1))
        def _():
            for p in across[:KEEP]:
                placed(g, p).start()

        @pl.when((g >= HELD) & (is_held | (half == 1)))
        def _():
            for p in across[KEEP:]:
                placed(g, p).start()

        for p in near:
            placed(g, p).start()
        kept(g).start()
        return carry

    lax.fori_loop(0, HK, group_step, 0)

    for g in range(HK):
        bvec[HK, g : g + 1] = colsum[g, 0, :1]
        bvec[HK, HK + g : HK + g + 1] = colsum[g, 1, :1]

    @pl.when(inner != HK + FIRST_OWNER)
    def _():
        to_owner(HK).start()

    mine = inner - FIRST_OWNER

    def to_x(j):
        return remote(b2.at[x], b2.at[x], p2_s.at[j], p2_r.at[x], along_x[j - 1])

    def from_x(j):
        at = lax.rem(x + j, 4)
        return remote(b2.at[at], b2.at[at], p2_s.at[j], p2_r.at[at], along_x[j - 1])

    def to_z(j):
        return remote(b3.at[depth], b3.at[depth], p3_s.at[j], p3_r.at[depth], along_z[j - 1])

    def from_z(j):
        at = lax.rem(depth + j, 8)
        return remote(b3.at[at], b3.at[at], p3_s.at[j], p3_r.at[at], along_z[j - 1])

    def to_near(j):
        device = {"ctx": near[j - 1]}
        return remote(btot.at[mine], btot.at[mine], p4_s.at[j], p4_r.at[mine], device)

    with scope("owner"):

        @pl.when(is_owner)
        def _():
            b1[inner] = bvec[mine]
            for j in range(1, 8):
                at = lax.rem(inner + j, 8)
                remote(
                    bvec.at[mine], b1.at[at], p1_s.at[mine], p1_r.at[at], {"ctx": near[j - 1]}
                ).wait_recv()
            total = b1[0]
            for j in range(1, 8):
                total = total + b1[j]
            b2[x] = total
            for j in range(1, 4):
                to_x(j).start()
            for j in range(1, 4):
                from_x(j).wait_recv()
            b3[depth] = (b2[0] + b2[1]) + (b2[2] + b2[3])
            for j in range(1, 8):
                to_z(j).start()

    with scope("relay"):

        @pl.when(is_back_relay)
        def _():
            term_to_relay(0, 0).wait_recv()
            term_relayed(0).start()

            @pl.when(core == 0)
            def _():
                term_to_relay(0, 1).wait_recv()
                term_relayed(1).start()

    @pl.when(is_held)
    def _():
        for g in range(HELD, HK):
            for p in across[:KEEP]:
                placed(g, p).start()

    with scope("total"):

        @pl.when(is_owner)
        def _():
            for j in range(1, 8):
                from_z(j).wait_recv()
            total = b3[0]
            for j in range(1, 8):
                total = total + b3[j]
            btot[mine] = total
            for j in range(1, 8):
                to_near(j).start()

    with scope("bias"):
        for s in range(SLICES):

            @pl.when(inner != s + FIRST_OWNER)
            def _():
                remote(
                    btot.at[s], btot.at[s], p4_s.at[0], p4_r.at[s],
                    {"ctx": half * 8 + s + FIRST_OWNER},
                ).wait_recv()

    bias_ref[...] = btot[...]

    with scope("gkv"):
        for g in range(HK):
            for slot in (1, 0):

                @pl.when(me + (2 - slot) < N)
                def _():
                    term(g, slot).wait_recv()

                @pl.when(me + (2 - slot) >= N)
                def _():
                    part_in[g, slot] = jnp.zeros((2, ROWS, HD), jnp.bfloat16)

            for i in range(2):
                total = own[g, i] + part_in[g, 1, i].astype(jnp.float32)
                total = total + part_in[g, 0, i].astype(jnp.float32)
                gkv[:, i, :, g * HD : (g + 1) * HD] = total.reshape(N, BLK, HD).astype(
                    jnp.bfloat16
                )
        result = pltpu.make_async_copy(gkv, rows_ref.at[:, :, :, HQ * HD :], gkv_s)
        result.start()

    def finish(g, carry):
        for slot in (1, 0):

            @pl.when(has_next(g, slot))
            def _():
                halo(g, slot).wait_send()

            @pl.when(has_before(g, slot))
            def _():
                term(g, slot).wait_send()

            @pl.when(returns(slot) & (g < HK - 1))
            def _():
                term_to_relay(g, slot).wait_send()

        @pl.when((half == 0) & (column == HK - 1) & (g > 0))
        def _():
            to_relay(g).wait_send()

        @pl.when(me == 8)
        def _():
            handed(g).wait_send()

        @pl.when(inner != g + FIRST_OWNER)
        def _():
            to_owner(g).wait_send()

        kept(g).wait()
        for p in near:
            placed(g, p).wait_send()
        for p in near:
            arrived(g, p).wait_recv()

        @pl.when(g == 0)
        def _():
            for part in range(2):
                for p in across:
                    early(part, p, me).wait_send()
                for p in across:
                    early(part, p, p).wait_recv()

        @pl.when(g > 0)
        def _():
            for p in across:
                placed(g, p).wait_send()
            for p in across:
                arrived(g, p).wait_recv()

        return carry

    with scope("finish"):
        lax.fori_loop(0, HK, finish, 0)
        result.wait()

    @pl.when(inner != HK + FIRST_OWNER)
    def _():
        to_owner(HK).wait_send()

    @pl.when(is_relay)
    def _():
        relayed().wait_send()

    @pl.when(is_back_relay)
    def _():
        term_relayed(0).wait_send()

        @pl.when(core == 0)
        def _():
            term_relayed(1).wait_send()

    @pl.when(is_owner)
    def _():
        for j in range(1, 4):
            to_x(j).wait_send()
        for j in range(1, 8):
            to_z(j).wait_send()
            to_near(j).wait_send()


PARTS = 4


def lay_out(rows_ref, bias_ref, attn_ref, gq_ref, gk_ref, gv_ref, gb_ref, held, bias, in_s, out_s):
    wide = slice(0, HQ * HD)
    narrow = slice(HQ * HD, (HQ + HK) * HD)
    size = N // PARTS
    first = [pltpu.make_async_copy(bias_ref, bias, in_s.at[PARTS])]
    for i in range(PARTS):
        at = slice(i * size, (i + 1) * size)
        first.append(pltpu.make_async_copy(rows_ref.at[at], held.at[at], in_s.at[i]))
    for copy in first:
        copy.start()
    first[0].wait()
    then = [pltpu.make_async_copy(bias, gb_ref, out_s.at[PARTS, 0])]
    then[0].start()
    for i in range(PARTS):
        at = slice(i * size, (i + 1) * size)
        first[1 + i].wait()
        for n, (which, cols, ref) in enumerate(
            ((0, wide, attn_ref), (1, wide, gq_ref), (0, narrow, gk_ref), (1, narrow, gv_ref))
        ):
            copy = pltpu.make_async_copy(held.at[at, which, :, cols], ref.at[at], out_s.at[i, n])
            copy.start()
            then.append(copy)
    for copy in then:
        copy.wait()


def local(queries, keys, values, grad_out, doc_lengths, placement):
    vmem = pl.BlockSpec(memory_space=pltpu.VMEM)
    bf16, f32 = jnp.bfloat16, jnp.float32
    dma = pltpu.SemaphoreType.DMA
    rows, bias = pl.pallas_call(
        kernel,
        out_shape=(
            jax.ShapeDtypeStruct((N, 2, BLK, (HQ + HK) * HD), bf16),
            jax.ShapeDtypeStruct((SLICES, 8, HD), f32),
        ),
        in_specs=[pl.BlockSpec(memory_space=pltpu.HBM)] * 6,
        out_specs=(pl.BlockSpec(memory_space=pl.ANY), vmem),
        scratch_shapes=[
            pltpu.SMEM((1, N), jnp.int32),
            pltpu.SMEM((1, N, N), jnp.int32),
            pltpu.VMEM((ROWS, HQ * HD), bf16),
            pltpu.VMEM((ROWS, HK * HD), bf16),
            pltpu.VMEM((ROWS, HK * HD), bf16),
            pltpu.VMEM((ROWS, HQ * HD), bf16),
            dma((2 * HK + 4,)),
            pltpu.VMEM((N, 2, BLK, HK * HD), bf16),
            dma,
            pltpu.VMEM((HK, 3, 2, ROWS, HD), bf16),
            pltpu.VMEM((2, ROWS, HD), bf16),
            pltpu.VMEM((N, 2, BLK, HQ * HD), bf16),
            pltpu.VMEM((ROWS, ROWS), bf16),
            pltpu.VMEM((WIN, ROWS), f32),
            pltpu.VMEM((WIN, GROUP * ROWS), bf16),
            pltpu.VMEM((WIN, GROUP * ROWS), bf16),
            pltpu.VMEM((GROUP * ROWS, HD), bf16),
            pltpu.VMEM((HK, 2, 2, ROWS, HD), bf16),
            pltpu.VMEM((HK, 2, 2, ROWS, HD), bf16),
            pltpu.VMEM((2, 2, ROWS, HD), bf16),
            pltpu.VMEM((HK, 2, ROWS, HD), f32),
            pltpu.VMEM((HK, 2, 8, HD), f32),
            pltpu.VMEM((SLICES, 8, HD), f32),
            pltpu.VMEM((8, 8, HD), f32),
            pltpu.VMEM((4, 8, HD), f32),
            pltpu.VMEM((8, 8, HD), f32),
            pltpu.VMEM((SLICES, 8, HD), f32),
            dma((HK, 2)), dma((HK, 2)), dma((HK,)), dma((1,)), dma((1,)), dma((2,)), dma((2,)),
            dma((HK + 1, N)), dma((HK + 1, N)), dma((HK,)),
            dma((HK, 2)), dma((HK, 2)),
            dma((SLICES,)), dma((8,)), dma((4,)), dma((4,)),
            dma((8,)), dma((8,)), dma((8,)), dma((SLICES,)),
        ],
        compiler_params=pltpu.CompilerParams(
            collective_id=0, has_side_effects=True, vmem_limit_bytes=60 * 1024 * 1024
        ),
        cost_estimate=pl.CostEstimate(
            flops=2 * 6 * ROWS * HQ * HD * WIN,
            bytes_accessed=6 * 1024 * 1024,
            transcendentals=ROWS * HQ * WIN,
        ),
    )(doc_lengths, placement, queries[0], keys[0], values[0], grad_out[0])
    shape = jax.ShapeDtypeStruct
    results = pl.pallas_call(
        lay_out,
        out_shape=(
            shape((N, BLK, HQ * HD), bf16),
            shape((N, BLK, HQ * HD), bf16),
            shape((N, BLK, HK * HD), bf16),
            shape((N, BLK, HK * HD), bf16),
            shape((SLICES, 8, HD), f32),
        ),
        in_specs=[pl.BlockSpec(memory_space=pl.ANY)] * 2,
        out_specs=(pl.BlockSpec(memory_space=pl.ANY),) * 5,
        scratch_shapes=[
            pltpu.VMEM((N, 2, BLK, (HQ + HK) * HD), bf16),
            pltpu.VMEM((SLICES, 8, HD), f32),
            dma((PARTS + 1,)),
            dma((PARTS + 1, 4)),
        ],
        compiler_params=pltpu.CompilerParams(vmem_limit_bytes=60 * 1024 * 1024),
        cost_estimate=pl.CostEstimate(flops=0, bytes_accessed=5 * 1024 * 1024, transcendentals=0),
    )(rows, bias)
    return (
        results[0].reshape(1, ROWS, HQ * HD),
        results[1].reshape(1, ROWS, HQ * HD),
        results[2].reshape(1, ROWS, HK * HD),
        results[3].reshape(1, ROWS, HK * HD),
        results[4].reshape(SLICES * 8 * HD),
    )


def solution(mesh):
    return jax.shard_map(
        local,
        mesh=mesh,
        in_specs=(
            P("dp", "ctx", None),
            P("dp", "ctx", None),
            P("dp", "ctx", None),
            P("dp", "ctx", None),
            P("dp", None),
            P("dp", None, None),
        ),
        out_specs=(
            P("dp", "ctx", None),
            P("dp", "ctx", None),
            P("dp", "ctx", None),
            P("dp", "ctx", None),
            P(),
        ),
        check_vma=False,
    )
```

```python
import contextlib
import math

import jax
import jax.numpy as jnp
from jax import lax
from jax.experimental import pallas as pl
from jax.experimental.pallas import tpu as pltpu
from jax.sharding import PartitionSpec as P

HD = 128
HQ = 32
HK = 4
GROUP = HQ // HK
ROWS = 128
WIN = 384
BLK = 8
N = 16
MESH = pl.DeviceIdType.MESH
NT = (((1,), (1,)), ((), ()))
SCALE = 1.0 / math.sqrt(HD)
LOG2E = math.log2(math.e)
SLICES = HK + 1
FIRST_OWNER = 2
HELD = 3
KEEP = 4
EARLY = 2 * HD


SCOPES = False


def scope(name):
    return jax.named_scope(name) if SCOPES else contextlib.nullcontext()


def dot(a, b):
    return jnp.dot(a, b, preferred_element_type=jnp.float32)


def dot_nt(a, b):
    return lax.dot_general(a, b, NT, preferred_element_type=jnp.float32)


def halves(x):
    high = x.astype(jnp.bfloat16)
    return high, (x - high.astype(jnp.float32)).astype(jnp.bfloat16)


def kernel(
    len_hbm, place_hbm, q_hbm, k_hbm, v_hbm, do_hbm,
    rows_ref, bias_ref,
    len_ref, place_ref, q_ref, k_ref, v_ref, do_ref, in_s, gkv, gkv_s, win, win_relay, send, perm, mask,
    probs, dscore, ones, part, part_in, part_relay, own, colsum, bvec, b1, b2, b3, btot,
    halo_s, halo_r, pass_s, relay_s, relay_r, back_s, back_r, a2a_s, a2a_r, loc_s, part_s, part_r,
    p1_s, p1_r, p2_s, p2_r, p3_s, p3_r, p4_s, p4_r,
):
    me = lax.axis_index("ctx")
    seq = lax.axis_index("dp")
    half = me // 8
    inner = lax.rem(me, 8)

    x = seq // 4
    low = lax.rem(seq, 4)
    depth = half * 4 + low
    core = lax.rem(me, 2)

    across = [(1 - half) * 8 + lax.rem(inner + j, 8) for j in range(8)]
    near = [half * 8 + lax.rem(inner + j, 8) for j in range(1, 8)]
    peers = [{"ctx": p} for p in across + near]
    along_x = [{"dp": lax.rem(x + j, 4) * 4 + low} for j in range(1, 4)]
    along_z = []
    for j in range(1, 8):
        z = lax.rem(depth + j, 8)
        along_z.append({"ctx": (z // 4) * 8 + inner, "dp": x * 4 + lax.rem(z, 4)})
    others = peers + along_x + [along_z[j - 1] for j in range(1, 8) if j != 4]

    def remote(src, dst, send_sem, recv_sem, device):
        return pltpu.make_async_remote_copy(
            src_ref=src, dst_ref=dst, send_sem=send_sem, recv_sem=recv_sem,
            device_id=device, device_id_type=MESH,
        )

    def columns(g):
        return pl.ds(pl.multiple_of(g * GROUP * HD, GROUP * HD), GROUP * HD)

    def fetch_q(g):
        return pltpu.make_async_copy(q_hbm.at[:, columns(g)], q_ref.at[:, columns(g)], in_s.at[g])

    def fetch_do(g):
        return pltpu.make_async_copy(
            do_hbm.at[:, columns(g)], do_ref.at[:, columns(g)], in_s.at[HK + g]
        )

    small = [
        pltpu.make_async_copy(src, dst, in_s.at[2 * HK + i])
        for i, (src, dst) in enumerate(
            ((k_hbm, k_ref), (v_hbm, v_ref), (len_hbm, len_ref), (place_hbm, place_ref))
        )
    ]
    with scope("signals"):
        for copy in small:
            copy.start()
        barrier = pltpu.get_barrier_semaphore()
        for device in others:
            pl.semaphore_signal(barrier, inc=1, device_id=device, device_id_type=MESH)
        for g in range(HK):
            fetch_q(g).start()
            fetch_do(g).start()
        for copy in small:
            copy.wait()

    for g in range(HK):
        win[g, 2, 0] = k_ref[:, g * HD : (g + 1) * HD]
        win[g, 2, 1] = v_ref[:, g * HD : (g + 1) * HD]

    @pl.when(me < 2)
    def _():
        win[:, 0] = jnp.zeros((HK, 2, ROWS, HD), jnp.bfloat16)

    @pl.when(me < 1)
    def _():
        win[:, 1] = jnp.zeros((HK, 2, ROWS, HD), jnp.bfloat16)

    with scope("barrier"):
        pl.semaphore_wait(barrier, len(others))

    def halo(g, slot):
        return remote(
            win.at[g, 2], win.at[g, slot], halo_s.at[g, slot], halo_r.at[g, slot],
            {"ctx": lax.rem(me + (2 - slot), N)},
        )

    def term(g, slot):
        return remote(
            part.at[g, slot], part_in.at[g, slot], part_s.at[g, slot], part_r.at[g, slot],
            {"ctx": lax.rem(me + N - (2 - slot), N)},
        )

    column = inner // 2
    relay_head = HK - 1 - column

    def leaves(slot):
        return (half == 0) & (me + (2 - slot) >= 8)

    def returns(slot):
        return (half == 1) & (me - (2 - slot) < 8)

    def has_next(g, slot):
        direct = jnp.logical_not(leaves(slot)) | ((g == 0) & (inner == 6 + slot))
        return (me + (2 - slot) < N) & direct

    def to_relay(g):
        return remote(
            win.at[g, 2], win_relay, halo_s.at[g, 0], relay_r.at[0],
            {"ctx": 2 * (HK - 1 - g) + core},
        )

    def relayed():
        return remote(
            win_relay, win.at[relay_head, core], relay_s.at[0], halo_r.at[relay_head, core],
            {"ctx": 8},
        )

    def handed(g):
        return remote(
            win.at[g, 1], win.at[g, 0], pass_s.at[g], halo_r.at[g, 0], {"ctx": 9}
        )

    is_relay = (half == 0) & (column < HK - 1)

    with scope("halo_start"):
        for g in range(HK):
            for slot in (1, 0):

                @pl.when(has_next(g, slot))
                def _():
                    halo(g, slot).start()

            if g > 0:

                @pl.when((half == 0) & (column == HK - 1))
                def _():
                    to_relay(g).start()

    lane = lax.broadcasted_iota(jnp.int32, (1, ROWS), 1)
    pos = me * ROWS + lane
    first = jnp.zeros((1, ROWS), jnp.int32)
    start = len_ref[0, 0] * 0
    for i in range(N):
        first = jnp.where(pos >= start, start, first)
        start = start + len_ref[0, i]
    t_pos = (me - 2) * ROWS + lax.broadcasted_iota(jnp.int32, (WIN, ROWS), 0)
    seen = (t_pos >= first) & (t_pos <= pos)
    mask[...] = jnp.where(seen, 0.0, -1e30)

    target = lax.rem(lane, BLK)
    for j in range(N):
        target = target + jnp.where(lane // BLK == j, place_ref[0, me, j] * BLK, 0)
    row = lax.broadcasted_iota(jnp.int32, (ROWS, ROWS), 0)
    perm[...] = jnp.where(row == target, 1.0, 0.0).astype(jnp.bfloat16)
    ones[...] = jnp.where(
        lax.broadcasted_iota(jnp.int32, (GROUP * ROWS, HD), 0) // ROWS
        == lax.broadcasted_iota(jnp.int32, (GROUP * ROWS, HD), 1),
        1.0, 0.0,
    ).astype(jnp.bfloat16)

    @pl.when(is_relay)
    def _():
        to_relay(1).wait_recv()
        relayed().start()

    def has_before(g, slot):
        return (me >= 2 - slot) & (jnp.logical_not(returns(slot)) | (g == HK - 1))

    def term_to_relay(g, slot):
        return remote(
            part.at[g, slot], part_relay.at[slot], part_s.at[g, slot], back_r.at[slot],
            {"ctx": 8 + 2 * (HK - 1 - g) + core},
        )

    def term_relayed(slot):
        return remote(
            part_relay.at[slot], part_in.at[relay_head, slot], back_s.at[slot],
            part_r.at[relay_head, slot], {"ctx": 8 + core - (2 - slot)},
        )

    is_back_relay = (half == 1) & (column > 0)

    def placed(g, p):
        cols = columns(g)
        return remote(
            send.at[p, :, :, cols], rows_ref.at[me, :, :, cols], a2a_s.at[g, p], a2a_r.at[g, me],
            {"ctx": p},
        )

    def arrived(g, p):
        cols = columns(g)
        return remote(
            send.at[p, :, :, cols], rows_ref.at[p, :, :, cols], a2a_s.at[g, p], a2a_r.at[g, p],
            {"ctx": p},
        )

    def early(part, p, source):
        cols = (slice(0, EARLY), slice(EARLY, GROUP * HD))[part]
        i = (HK, 0)[part]
        return remote(
            send.at[p, :, :, cols], rows_ref.at[source, :, :, cols], a2a_s.at[i, p],
            a2a_r.at[i, source], {"ctx": p},
        )

    def kept(g):
        cols = columns(g)
        return pltpu.make_async_copy(
            send.at[me, :, :, cols], rows_ref.at[me, :, :, cols], loc_s.at[g]
        )

    def to_owner(s):
        return remote(
            bvec.at[s], b1.at[inner], p1_s.at[s], p1_r.at[inner],
            {"ctx": half * 8 + s + FIRST_OWNER},
        )

    is_owner = (inner >= FIRST_OWNER) & (inner < FIRST_OWNER + SLICES)
    is_held = inner >= 2

    def group_step(g, carry):
        with scope("halo"):
            fetch_q(g).wait()
            fetch_do(g).wait()
            for slot in (1, 0):

                @pl.when(me >= 2 - slot)
                def _():
                    halo(g, slot).wait_recv()

                if slot == 1:

                    @pl.when(me == 8)
                    def _():
                        handed(g).start()

        keys = win[g, :, 0].reshape(WIN, HD)
        values = win[g, :, 1].reshape(WIN, HD)
        keys_t = keys.astype(jnp.float32).T.astype(jnp.bfloat16)
        values_t = values.astype(jnp.float32).T.astype(jnp.bfloat16)
        shut = jnp.concatenate([mask[...], mask[...]], axis=1)

        def stacked(ref, first_head, count):
            cols = pl.ds(pl.multiple_of((g * GROUP + first_head) * HD, HD), count * HD)
            x = ref[:, cols]
            return jnp.concatenate([x[:, i * HD : (i + 1) * HD] for i in range(count)], axis=0)

        with scope("heads"):
            def products(pair):
                q2 = stacked(q_ref, pair * 2, 2)
                do2 = stacked(do_ref, pair * 2, 2)
                return dot_nt(keys, q2) + shut, dot_nt(values, do2)

            ahead = products(0)
            for pair in range(GROUP // 2):
                scores, grad = ahead
                if pair + 1 < GROUP // 2:
                    ahead = products(pair + 1)
                top = jnp.max(scores, axis=0, keepdims=True)
                e = jnp.exp2((scores - top) * (SCALE * LOG2E))
                inv = 1.0 / jnp.sum(e, axis=0, keepdims=True)
                weights = (e * inv).astype(jnp.bfloat16)
                delta = jnp.sum(weights.astype(jnp.float32) * grad, axis=0, keepdims=True)
                ds = (e * (inv * SCALE) * (grad - delta)).astype(jnp.bfloat16)
                at = slice(pair * 2 * ROWS, (pair + 1) * 2 * ROWS)
                probs[:, at] = weights
                dscore[:, at] = ds
                cols = pl.ds(pl.multiple_of((g * GROUP + pair * 2) * HD, 2 * HD), 2 * HD)
                for i, out_t in enumerate((dot(values_t, weights), dot(keys_t, ds))):
                    out_t = out_t.astype(jnp.bfloat16)
                    out = dot_nt(
                        perm[...], jnp.concatenate([out_t[:, :ROWS], out_t[:, ROWS:]], axis=0)
                    )
                    send[:, i, :, cols] = out.reshape(N, BLK, 2 * HD).astype(jnp.bfloat16)

                if (pair + 1) * 2 * HD == EARLY:

                    @pl.when(g == 0)
                    def _():
                        for p in across:
                            early(0, p, me).start()

        with scope("sends"):

            @pl.when(g == 0)
            def _():
                for p in across:
                    early(1, p, me).start()

            @pl.when((g > 0) & ((g < HELD) | jnp.logical_not(is_held | (half == 1))))
            def _():
                for p in across:
                    placed(g, p).start()


        with scope("terms"):
            dv = dot(probs[...], stacked(do_ref, 0, GROUP))
            both = jnp.concatenate([stacked(q_ref, 0, GROUP), ones[...]], axis=1)
            dk = dot(dscore[...], both)
            part[g, :, 0] = dk[: 2 * ROWS, :HD].reshape(2, ROWS, HD).astype(jnp.bfloat16)
            part[g, :, 1] = dv[: 2 * ROWS].reshape(2, ROWS, HD).astype(jnp.bfloat16)
            for slot in (1, 0):

                @pl.when(has_before(g, slot))
                def _():
                    term(g, slot).start()

                @pl.when(returns(slot) & (g < HK - 1))
                def _():
                    term_to_relay(g, slot).start()

            own[g, 0] = dk[2 * ROWS :, :HD]
            own[g, 1] = dv[2 * ROWS :]
            colsum[g, 0] = jnp.broadcast_to(jnp.sum(dk[:, :HD], axis=0, keepdims=True), (8, HD))
            colsum[g, 1] = jnp.broadcast_to(jnp.sum(dv, axis=0, keepdims=True), (8, HD))
            high, low = halves(dk[:, HD:])
            query_sum = dot(keys_t, high) + dot(keys_t, low)
            bvec[g] = query_sum.T[:GROUP]

            @pl.when(inner != g + FIRST_OWNER)
            def _():
                to_owner(g).start()

        @pl.when((g >= HELD) & jnp.logical_not(is_held) & (half == 1))
        def _():
            for p in across[:KEEP]:
                placed(g, p).start()

        @pl.when((g >= HELD) & (is_held | (half == 1)))
        def _():
            for p in across[KEEP:]:
                placed(g, p).start()

        for p in near:
            placed(g, p).start()
        kept(g).start()
        return carry

    lax.fori_loop(0, HK, group_step, 0)

    for g in range(HK):
        bvec[HK, g : g + 1] = colsum[g, 0, :1]
        bvec[HK, HK + g : HK + g + 1] = colsum[g, 1, :1]

    @pl.when(inner != HK + FIRST_OWNER)
    def _():
        to_owner(HK).start()

    mine = inner - FIRST_OWNER

    def to_x(j):
        return remote(b2.at[x], b2.at[x], p2_s.at[j], p2_r.at[x], along_x[j - 1])

    def from_x(j):
        at = lax.rem(x + j, 4)
        return remote(b2.at[at], b2.at[at], p2_s.at[j], p2_r.at[at], along_x[j - 1])

    def to_z(j):
        return remote(b3.at[depth], b3.at[depth], p3_s.at[j], p3_r.at[depth], along_z[j - 1])

    def from_z(j):
        at = lax.rem(depth + j, 8)
        return remote(b3.at[at], b3.at[at], p3_s.at[j], p3_r.at[at], along_z[j - 1])

    def to_near(j):
        device = {"ctx": near[j - 1]}
        return remote(btot.at[mine], btot.at[mine], p4_s.at[j], p4_r.at[mine], device)

    with scope("owner"):

        @pl.when(is_owner)
        def _():
            b1[inner] = bvec[mine]
            for j in range(1, 8):
                at = lax.rem(inner + j, 8)
                remote(
                    bvec.at[mine], b1.at[at], p1_s.at[mine], p1_r.at[at], {"ctx": near[j - 1]}
                ).wait_recv()
            total = b1[0]
            for j in range(1, 8):
                total = total + b1[j]
            b2[x] = total
            for j in range(1, 4):
                to_x(j).start()
            for j in range(1, 4):
                from_x(j).wait_recv()
            b3[depth] = (b2[0] + b2[1]) + (b2[2] + b2[3])
            for j in range(1, 8):
                to_z(j).start()

    with scope("relay"):

        @pl.when(is_back_relay)
        def _():
            term_to_relay(0, 0).wait_recv()
            term_relayed(0).start()

            @pl.when(core == 0)
            def _():
                term_to_relay(0, 1).wait_recv()
                term_relayed(1).start()

    @pl.when(is_held)
    def _():
        for g in range(HELD, HK):
            for p in across[:KEEP]:
                placed(g, p).start()

    with scope("total"):

        @pl.when(is_owner)
        def _():
            for j in range(1, 8):
                from_z(j).wait_recv()
            total = b3[0]
            for j in range(1, 8):
                total = total + b3[j]
            btot[mine] = total
            for j in range(1, 8):
                to_near(j).start()

    with scope("bias"):
        for s in range(SLICES):

            @pl.when(inner != s + FIRST_OWNER)
            def _():
                remote(
                    btot.at[s], btot.at[s], p4_s.at[0], p4_r.at[s],
                    {"ctx": half * 8 + s + FIRST_OWNER},
                ).wait_recv()

    bias_ref[...] = btot[...]

    with scope("gkv"):
        for g in range(HK):
            for slot in (1, 0):

                @pl.when(me + (2 - slot) < N)
                def _():
                    term(g, slot).wait_recv()

                @pl.when(me + (2 - slot) >= N)
                def _():
                    part_in[g, slot] = jnp.zeros((2, ROWS, HD), jnp.bfloat16)

            for i in range(2):
                total = own[g, i] + part_in[g, 1, i].astype(jnp.float32)
                total = total + part_in[g, 0, i].astype(jnp.float32)
                gkv[:, i, :, g * HD : (g + 1) * HD] = total.reshape(N, BLK, HD).astype(
                    jnp.bfloat16
                )
        result = pltpu.make_async_copy(gkv, rows_ref.at[:, :, :, HQ * HD :], gkv_s)
        result.start()

    def finish(g, carry):
        for slot in (1, 0):

            @pl.when(has_next(g, slot))
            def _():
                halo(g, slot).wait_send()

            @pl.when(has_before(g, slot))
            def _():
                term(g, slot).wait_send()

            @pl.when(returns(slot) & (g < HK - 1))
            def _():
                term_to_relay(g, slot).wait_send()

        @pl.when((half == 0) & (column == HK - 1) & (g > 0))
        def _():
            to_relay(g).wait_send()

        @pl.when(me == 8)
        def _():
            handed(g).wait_send()

        @pl.when(inner != g + FIRST_OWNER)
        def _():
            to_owner(g).wait_send()

        kept(g).wait()
        for p in near:
            placed(g, p).wait_send()
        for p in near:
            arrived(g, p).wait_recv()

        @pl.when(g == 0)
        def _():
            for part in range(2):
                for p in across:
                    early(part, p, me).wait_send()
                for p in across:
                    early(part, p, p).wait_recv()

        @pl.when(g > 0)
        def _():
            for p in across:
                placed(g, p).wait_send()
            for p in across:
                arrived(g, p).wait_recv()

        return carry

    with scope("finish"):
        lax.fori_loop(0, HK, finish, 0)
        result.wait()

    @pl.when(inner != HK + FIRST_OWNER)
    def _():
        to_owner(HK).wait_send()

    @pl.when(is_relay)
    def _():
        relayed().wait_send()

    @pl.when(is_back_relay)
    def _():
        term_relayed(0).wait_send()

        @pl.when(core == 0)
        def _():
            term_relayed(1).wait_send()

    @pl.when(is_owner)
    def _():
        for j in range(1, 4):
            to_x(j).wait_send()
        for j in range(1, 8):
            to_z(j).wait_send()
            to_near(j).wait_send()


PARTS = 4


def lay_out(rows_ref, bias_ref, attn_ref, gq_ref, gk_ref, gv_ref, gb_ref, held, bias, in_s, out_s):
    wide = slice(0, HQ * HD)
    narrow = slice(HQ * HD, (HQ + HK) * HD)
    size = N // PARTS
    first = [pltpu.make_async_copy(bias_ref, bias, in_s.at[PARTS])]
    for i in range(PARTS):
        at = slice(i * size, (i + 1) * size)
        first.append(pltpu.make_async_copy(rows_ref.at[at], held.at[at], in_s.at[i]))
    for copy in first:
        copy.start()
    first[0].wait()
    then = [pltpu.make_async_copy(bias, gb_ref, out_s.at[PARTS, 0])]
    then[0].start()
    for i in range(PARTS):
        at = slice(i * size, (i + 1) * size)
        first[1 + i].wait()
        for n, (which, cols, ref) in enumerate(
            ((0, wide, attn_ref), (1, wide, gq_ref), (0, narrow, gk_ref), (1, narrow, gv_ref))
        ):
            copy = pltpu.make_async_copy(held.at[at, which, :, cols], ref.at[at], out_s.at[i, n])
            copy.start()
            then.append(copy)
    for copy in then:
        copy.wait()


def local(queries, keys, values, grad_out, doc_lengths, placement):
    vmem = pl.BlockSpec(memory_space=pltpu.VMEM)
    bf16, f32 = jnp.bfloat16, jnp.float32
    dma = pltpu.SemaphoreType.DMA
    rows, bias = pl.pallas_call(
        kernel,
        out_shape=(
            jax.ShapeDtypeStruct((N, 2, BLK, (HQ + HK) * HD), bf16),
            jax.ShapeDtypeStruct((SLICES, 8, HD), f32),
        ),
        in_specs=[pl.BlockSpec(memory_space=pltpu.HBM)] * 6,
        out_specs=(pl.BlockSpec(memory_space=pl.ANY), vmem),
        scratch_shapes=[
            pltpu.SMEM((1, N), jnp.int32),
            pltpu.SMEM((1, N, N), jnp.int32),
            pltpu.VMEM((ROWS, HQ * HD), bf16),
            pltpu.VMEM((ROWS, HK * HD), bf16),
            pltpu.VMEM((ROWS, HK * HD), bf16),
            pltpu.VMEM((ROWS, HQ * HD), bf16),
            dma((2 * HK + 4,)),
            pltpu.VMEM((N, 2, BLK, HK * HD), bf16),
            dma,
            pltpu.VMEM((HK, 3, 2, ROWS, HD), bf16),
            pltpu.VMEM((2, ROWS, HD), bf16),
            pltpu.VMEM((N, 2, BLK, HQ * HD), bf16),
            pltpu.VMEM((ROWS, ROWS), bf16),
            pltpu.VMEM((WIN, ROWS), f32),
            pltpu.VMEM((WIN, GROUP * ROWS), bf16),
            pltpu.VMEM((WIN, GROUP * ROWS), bf16),
            pltpu.VMEM((GROUP * ROWS, HD), bf16),
            pltpu.VMEM((HK, 2, 2, ROWS, HD), bf16),
            pltpu.VMEM((HK, 2, 2, ROWS, HD), bf16),
            pltpu.VMEM((2, 2, ROWS, HD), bf16),
            pltpu.VMEM((HK, 2, ROWS, HD), f32),
            pltpu.VMEM((HK, 2, 8, HD), f32),
            pltpu.VMEM((SLICES, 8, HD), f32),
            pltpu.VMEM((8, 8, HD), f32),
            pltpu.VMEM((4, 8, HD), f32),
            pltpu.VMEM((8, 8, HD), f32),
            pltpu.VMEM((SLICES, 8, HD), f32),
            dma((HK, 2)), dma((HK, 2)), dma((HK,)), dma((1,)), dma((1,)), dma((2,)), dma((2,)),
            dma((HK + 1, N)), dma((HK + 1, N)), dma((HK,)),
            dma((HK, 2)), dma((HK, 2)),
            dma((SLICES,)), dma((8,)), dma((4,)), dma((4,)),
            dma((8,)), dma((8,)), dma((8,)), dma((SLICES,)),
        ],
        compiler_params=pltpu.CompilerParams(
            collective_id=0, has_side_effects=True, vmem_limit_bytes=60 * 1024 * 1024
        ),
        cost_estimate=pl.CostEstimate(
            flops=2 * 6 * ROWS * HQ * HD * WIN,
            bytes_accessed=6 * 1024 * 1024,
            transcendentals=ROWS * HQ * WIN,
        ),
    )(doc_lengths, placement, queries[0], keys[0], values[0], grad_out[0])
    shape = jax.ShapeDtypeStruct
    results = pl.pallas_call(
        lay_out,
        out_shape=(
            shape((N, BLK, HQ * HD), bf16),
            shape((N, BLK, HQ * HD), bf16),
            shape((N, BLK, HK * HD), bf16),
            shape((N, BLK, HK * HD), bf16),
            shape((SLICES, 8, HD), f32),
        ),
        in_specs=[pl.BlockSpec(memory_space=pl.ANY)] * 2,
        out_specs=(pl.BlockSpec(memory_space=pl.ANY),) * 5,
        scratch_shapes=[
            pltpu.VMEM((N, 2, BLK, (HQ + HK) * HD), bf16),
            pltpu.VMEM((SLICES, 8, HD), f32),
            dma((PARTS + 1,)),
            dma((PARTS + 1, 4)),
        ],
        compiler_params=pltpu.CompilerParams(vmem_limit_bytes=60 * 1024 * 1024),
        cost_estimate=pl.CostEstimate(flops=0, bytes_accessed=5 * 1024 * 1024, transcendentals=0),
    )(rows, bias)
    return (
        results[0].reshape(1, ROWS, HQ * HD),
        results[1].reshape(1, ROWS, HQ * HD),
        results[2].reshape(1, ROWS, HK * HD),
        results[3].reshape(1, ROWS, HK * HD),
        results[4].reshape(SLICES * 8 * HD),
    )


def solution(mesh):
    return jax.shard_map(
        local,
        mesh=mesh,
        in_specs=(
            P("dp", "ctx", None),
            P("dp", "ctx", None),
            P("dp", "ctx", None),
            P("dp", "ctx", None),
            P("dp", None),
            P("dp", None, None),
        ),
        out_specs=(
            P("dp", "ctx", None),
            P("dp", "ctx", None),
            P("dp", "ctx", None),
            P("dp", "ctx", None),
            P(),
        ),
        check_vma=False,
    )
```
